32 devices in a mesh: roi: 16 (over z, y, core), ch: 2 (over x).
Axes of the slice: x: 2, y: 2, z: 4, core: 2. Of those that a mesh axis runs over, the one named last changes fastest.
Arguments:
- pyramid_two: bfloat16 [32, 256, 4096], P('roi', 'ch'), may hold values from -6 to 6
- pyramid_three: bfloat16 [32, 256, 1024], P('roi', 'ch'), may hold values from -6 to 6
- pyramid_four: bfloat16 [32, 256, 256], P('roi', 'ch'), may hold values from -6 to 6
- pyramid_five: bfloat16 [32, 256, 64], P('roi', 'ch'), may hold values from -6 to 6
- proposals: float32 [4, 8192], P(None, 'roi'), may hold values from 0 to 1, as said below
- image_index: int32 [8192], P('roi'), may hold values from 0 to 31, as said below
- levels: int32 [8192], P('roi'), may hold values from 0 to 3
- labels: int32 [8192], P('roi'), may hold values from 0 to 80
- targets: float32 [4, 8192], P(None, 'roi'), may hold values from -6 to 6
- first_weight: bfloat16 [12544, 1024], P('ch'), may hold values from -0.0546875 to 0.0546875
- first_bias: bfloat16 [1024], replicated, may hold values from -3 to 3
- second_weight: bfloat16 [1024, 1024], replicated, may hold values from -0.1875 to 0.1875
- second_bias: bfloat16 [1024], replicated, may hold values from -3 to 3
- class_weight: bfloat16 [1024, 81], replicated, may hold values from -0.75 to 0.75
- class_bias: bfloat16 [81], replicated, may hold values from -4 to 4
- box_weight: bfloat16 [1024, 4], replicated, may hold values from -0.375 to 0.375
- box_bias: bfloat16 [4], replicated, may hold values from -3 to 3
Outputs:
- class_loss: float32 [], replicated
- box_loss: float32 [], replicated
- decoded: float32 [4, 8192], P(None, ('roi', 'ch'))
- first_weight_grad: float32 [12544, 1024], P('ch')
- first_bias_grad: float32 [1024], replicated
- second_weight_grad: float32 [1024, 1024], replicated
- second_bias_grad: float32 [1024], replicated
- class_weight_grad: float32 [1024, 81], replicated
- class_bias_grad: float32 [81], replicated
- box_weight_grad: float32 [1024, 4], replicated
- box_bias_grad: float32 [4], replicated
- pyramid_two_grad: float32 [32, 256, 4096], P('roi', 'ch')
- pyramid_three_grad: float32 [32, 256, 1024], P('roi', 'ch')
- pyramid_four_grad: float32 [32, 256, 256], P('roi', 'ch')
- pyramid_five_grad: float32 [32, 256, 64], P('roi', 'ch')
The draws below stay inside these ranges and needn't reach their ends.
Inputs may be any that keep to these rules, and one draw needn't show every extreme that they name: `proposals`: x1 < x2 and y1 < y2; every box is 1/64 of the image side wide and high or more. `image_index`: region r lies in one of the images 2 * (r // 512) to 2 * (r // 512) + 1; earlier images of such a group hold more regions.
All inputs are finite; a program needn't handle non-finite values.
Results may differ from the reference program's by a relative error of at most 0.0095.
Values may be sent and summed in bfloat16 or wider, within the bound.
No kernel may reach another device: no remote copies, remote signals or barrier semaphores. Data moves between devices by JAX's collectives and lax.ppermute only.
A program may use at most 256 MiB of HBM per device.

```python
import math
import jax
import jax.numpy as jnp
from jax import lax

CHANNELS = 256
HIDDEN_SIZE = 1024
CLASSES = 81
POOL = 7
SAMPLES = 2
FLAT = 12544
SIDE = 64
BLOCK = 128
IMG_DEV = 2
R_DEV = 512
IMAGES = 32
REGIONS = 8192


def draw_proposals(key, part):
    key = jax.random.fold_in(key, 11)
    subkeys = jax.random.split(key, 2)
    centres = jax.random.uniform(subkeys[0], (2, REGIONS), jnp.float32, 0.05, 0.95)
    extents = jnp.exp(jax.random.uniform(subkeys[1], (2, REGIONS), jnp.float32, math.log(1.0 / 32.0), math.log(0.5)))
    low_corner = jnp.clip(centres - 0.5 * extents, 0.0, 1.0)
    high_corner = jnp.clip(centres + 0.5 * extents, 0.0, 1.0)
    return jnp.concatenate([low_corner, high_corner], 0)


def draw_image_index(key, part):
    key = jax.random.fold_in(key, 23)
    subkeys = jax.random.split(key, 2)
    first_pick = jax.random.randint(subkeys[0], (REGIONS,), 0, IMG_DEV)
    second_pick = jax.random.randint(subkeys[1], (REGIONS,), 0, IMG_DEV)
    offset = jnp.minimum(first_pick, second_pick)
    rows = jnp.arange(REGIONS, dtype=jnp.int32)
    offset = jnp.where(rows % R_DEV == R_DEV - 1, IMG_DEV - 1, offset)
    offset = jnp.where(rows % R_DEV == 0, 0, offset)
    return rows // R_DEV * IMG_DEV + offset


def plant(entries, rng, least, largest):
    longest = entries.shape.index(max(entries.shape))
    spots = []
    for shift in (0, 1):
        where = [jax.random.randint(jax.random.fold_in(rng, axis), (), 0, length) for axis, length in enumerate(entries.shape)]
        where[longest] = (where[longest] + shift) % entries.shape[longest]
        spots.append(tuple(where))
    return entries.at[spots[0]].set(least).at[spots[1]].set(largest)


def shard_levels(key, dims, cuts, smallest, largest):
    def one(axis_at, parts):
        steps = jax.random.uniform(jax.random.fold_in(jax.random.fold_in(key, 6), axis_at), (parts,), jnp.float32, smallest / len(cuts), largest / len(cuts))
        return jnp.repeat(jnp.exp(steps), dims[axis_at] // parts).reshape((-1,) + (1,) * (len(dims) - axis_at - 1))

    factor_of = one(*cuts[0])
    for cut in cuts[1:]:
        factor_of = factor_of * one(*cut)
    return factor_of


def noise(stream_key, shape, width, limit, cuts=(), kind=jnp.bfloat16):
    array = width * jax.random.normal(stream_key, shape, jnp.float32)
    if cuts:
        array = array * shard_levels(stream_key, shape, cuts, -0.22, 0.18)
    return jnp.clip(array, -limit, limit).astype(kind)


def setup_inputs(seed: int = 0) -> dict:
    splits = jax.random.split(jax.random.key(seed), 18)
    return {
        "pyramid_two": noise(splits[0], (IMAGES, CHANNELS, SIDE * SIDE), 1.0, 6.0, ((0, 16), (1, 2))),
        "pyramid_three": noise(splits[1], (IMAGES, CHANNELS, SIDE * SIDE // 4), 1.0, 6.0, ((0, 16), (1, 2))),
        "pyramid_four": noise(splits[2], (IMAGES, CHANNELS, SIDE * SIDE // 16), 1.0, 6.0, ((0, 16), (1, 2))),
        "pyramid_five": noise(splits[3], (IMAGES, CHANNELS, SIDE * SIDE // 64), 1.0, 6.0, ((0, 16), (1, 2))),
        "proposals": draw_proposals(jax.random.fold_in(splits[17], 71), 0),
        "image_index": draw_image_index(jax.random.fold_in(splits[17], 71), 0),
        "levels": plant(jax.random.randint(splits[6], (REGIONS,), 0, 4), jax.random.fold_in(splits[6], 1), 0, 3).astype(jnp.int32),
        "labels": plant(jax.random.randint(splits[7], (REGIONS,), 0, CLASSES), jax.random.fold_in(splits[7], 1), 0, CLASSES - 1).astype(jnp.int32),
        "targets": noise(splits[8], (4, REGIONS), 1.0, 6.0, ((1, 16),), jnp.float32),
        "first_weight": noise(splits[9], (FLAT, HIDDEN_SIZE), FLAT ** -0.5, 0.0546875, ((0, 2),)),
        "first_bias": noise(splits[10], (HIDDEN_SIZE,), 0.5, 3.0),
        "second_weight": noise(splits[11], (HIDDEN_SIZE, HIDDEN_SIZE), HIDDEN_SIZE ** -0.5, 0.1875),
        "second_bias": noise(splits[12], (HIDDEN_SIZE,), 0.5, 3.0),
        "class_weight": noise(splits[13], (HIDDEN_SIZE, CLASSES), 64 ** -0.5, 0.75),
        "class_bias": noise(splits[14], (CLASSES,), 1.0, 4.0),
        "box_weight": noise(splits[15], (HIDDEN_SIZE, 4), 256 ** -0.5, 0.375),
        "box_bias": noise(splits[16], (4,), 0.5, 3.0),
    }


@jax.custom_vjp
def low(v):
    return lax.optimization_barrier(v.astype(jnp.bfloat16)).astype(jnp.float32)

@jax.custom_vjp
def low_back(v):
    return v

def low_keep(v):
    return (low(v), None)

def low_pass(kept, grad):
    return (grad,)

def back_keep(v):
    return (v, None)

def back_low(kept, grad):
    return (low(grad),)
low.defvjp(low_keep, low_pass)
low_back.defvjp(back_keep, back_low)

def smooth_unit(values):
    return jax.nn.gelu(values, approximate=False)

def spread_weights(low_edge, high_edge, extent):
    anchor = low_edge * extent - 0.5
    stride = (high_edge - low_edge) * extent / POOL
    columns = jnp.arange(POOL, dtype=jnp.float32)
    places = jnp.arange(extent, dtype=jnp.float32)
    weights = jnp.zeros((low_edge.shape[0], POOL, extent), jnp.float32)
    for sample in range(SAMPLES):
        located = anchor[:, None] + (columns[None, :] + (sample + 0.5) / SAMPLES) * stride[:, None]
        located = jnp.clip(located, 0.0, extent - 1.0)
        weights = weights + jnp.maximum(0.0, 1.0 - jnp.abs(located[:, :, None] - places[None, None, :]))
    return weights / SAMPLES

def level_tables(corners, local_image, level_ids, level_num, images_here):
    extent = SIDE // 2 ** level_num
    across = spread_weights(corners[0], corners[2], extent)
    downward = spread_weights(corners[1], corners[3], extent)
    picked = (local_image[:, None] == jnp.arange(images_here, dtype=jnp.int32)[None, :]) & (level_ids[:, None] == level_num)
    select = picked.astype(jnp.float32)[:, :, None, None] * across[:, None, :, :]
    select = jnp.transpose(select, (1, 3, 0, 2)).reshape(images_here * extent, -1)
    return (select, downward)

def as_matrix(feature, level_num):
    extent = SIDE // 2 ** level_num
    images_here, channels_here = (feature.shape[0], feature.shape[1])
    shaped = feature.reshape(images_here, channels_here, extent, extent).transpose(1, 2, 0, 3)
    return shaped.reshape(channels_here * extent, images_here * extent)

def pool_block(matrices, corners, local_image, level_ids):
    region_count = corners.shape[1]
    pooled_sum = jnp.zeros((region_count, CHANNELS, POOL, POOL), jnp.float32)
    for level_num in range(4):
        extent = SIDE // 2 ** level_num
        select, downward = level_tables(corners, local_image, level_ids, level_num, IMG_DEV)
        section_one = jnp.dot(matrices[level_num], low(select), precision=lax.Precision.HIGHEST)
        section_one = low_back(section_one).reshape(CHANNELS, extent, region_count, POOL)
        pooled_sum = pooled_sum + jnp.einsum('rih,chrj->rcij', downward, section_one, precision=lax.Precision.HIGHEST)
    return pooled_sum.reshape(region_count, -1)

def decode_boxes(corners, deltas):
    widths = corners[2] - corners[0]
    heights = corners[3] - corners[1]
    centre_x = corners[0] + 0.5 * widths
    centre_y = corners[1] + 0.5 * heights
    moved_x = deltas[:, 0] / 10.0 * widths + centre_x
    moved_y = deltas[:, 1] / 10.0 * heights + centre_y
    new_width = jnp.exp(deltas[:, 2] / 5.0) * widths
    new_height = jnp.exp(deltas[:, 3] / 5.0) * heights
    return jnp.stack([moved_x - 0.5 * new_width, moved_y - 0.5 * new_height, moved_x + 0.5 * new_width, moved_y + 0.5 * new_height])

def reference(pyramid_two, pyramid_three, pyramid_four, pyramid_five, proposals, image_index, levels, labels, targets, first_weight, first_bias, second_weight, second_bias, class_weight, class_bias, box_weight, box_bias):
    floats = tuple((item.astype(jnp.float32) for item in (pyramid_two, pyramid_three, pyramid_four, pyramid_five, first_weight, first_bias, second_weight, second_bias, class_weight, class_bias, box_weight, box_bias)))
    block_count = REGIONS // BLOCK
    block_ids = jnp.arange(block_count, dtype=jnp.int32)
    corner_blocks = proposals.reshape(4, block_count, BLOCK).transpose(1, 0, 2)
    image_blocks = image_index.reshape(block_count, BLOCK)
    level_blocks = levels.reshape(block_count, BLOCK)

    def forward(map_two, map_three, map_four, map_five, weight_one, bias_one, weight_two, bias_two, weight_class, bias_class, weight_box, bias_box):
        pyramids = (map_two, map_three, map_four, map_five)

        def one_block(pieces):
            block_id, corners, image_ids, level_ids = pieces
            first_image = (block_id * BLOCK // R_DEV * IMG_DEV).astype(jnp.int32)
            matrices = [as_matrix(lax.dynamic_slice_in_dim(pyramids[level_num], first_image, IMG_DEV, 0), level_num) for level_num in range(4)]
            return pool_block(matrices, corners, image_ids - first_image, level_ids)
        pooled = lax.map(jax.checkpoint(one_block), (block_ids, corner_blocks, image_blocks, level_blocks))
        pooled = low(low_back(pooled.reshape(REGIONS, FLAT)))
        pre_one = low_back(jnp.dot(pooled, weight_one, precision=lax.Precision.HIGHEST) + bias_one)
        act_one = low(smooth_unit(pre_one))
        pre_two = low_back(jnp.dot(act_one, weight_two, precision=lax.Precision.HIGHEST) + bias_two)
        act_two = low(smooth_unit(pre_two))
        logits = low_back(jnp.dot(act_two, weight_class, precision=lax.Precision.HIGHEST) + bias_class)
        deltas = low_back(jnp.dot(act_two, weight_box, precision=lax.Precision.HIGHEST) + bias_box)
        row_max = lax.optimization_barrier(jnp.max(logits, axis=1, keepdims=True))
        log_total = row_max[:, 0] + jnp.log(lax.optimization_barrier(jnp.sum(jnp.exp(logits - row_max), axis=1)))
        onehot = (labels[:, None] == jnp.arange(CLASSES, dtype=jnp.int32)[None, :]).astype(jnp.float32)
        class_loss = jnp.sum(log_total - lax.optimization_barrier(jnp.sum(logits * onehot, axis=1))) / REGIONS
        foreground = (labels < CLASSES - 1).astype(jnp.float32)[:, None]
        residue = deltas - targets.T
        magnitude = jnp.abs(residue)
        huber = jnp.where(magnitude < 1.0, 0.5 * residue * residue, magnitude - 0.5)
        box_loss = jnp.sum(foreground * huber) / REGIONS
        return (class_loss + box_loss, (class_loss, box_loss, deltas))
    overall, pullback, extras = jax.vjp(forward, *floats, has_aux=True)
    grads = pullback(jnp.ones_like(overall))
    class_loss, box_loss, deltas = extras
    decoded = decode_boxes(proposals, deltas)
    return (class_loss, box_loss, decoded, grads[4], grads[5], grads[6], grads[7], grads[8], grads[9], grads[10], grads[11], grads[0] / 3.0, grads[1] / 3.0, grads[2] / 3.0, grads[3] / 3.0)
```

```python
import functools
import jax, jax.numpy as jnp
from jax import lax
from jax.sharding import PartitionSpec as P
from jax.experimental import pallas as pl
from jax.experimental.pallas import tpu as pltpu

POOL = 7
SAMPLES = 2
SIDE = 64
LANES = 128
BF = jnp.bfloat16
F32 = jnp.float32
VM = 60 * 2**20


def spread(low, high, extent):
    anchor = low * extent - 0.5
    stride = (high - low) * extent / POOL
    places = lax.broadcasted_iota(jnp.int32, (extent, LANES), 0).astype(F32)
    out = []
    for col in range(POOL):
        total = None
        for s in range(SAMPLES):
            at = jnp.clip(anchor + (col + (s + 0.5) / SAMPLES) * stride, 0.0, extent - 1.0)
            term = jnp.maximum(0.0, 1.0 - jnp.abs(at - places))
            total = term if total is None else total + term
        out.append(total / SAMPLES)
    return out


def write_tables(across_ref, down_ref, rows, extent, level):
    x1, y1, x2, y2 = (rows[k : k + 1] for k in range(4))
    mask = (rows[9:10] == float(level)).astype(F32)
    across = spread(x1, x2, extent)
    down = spread(y1, y2, extent)
    for j in range(POOL):
        a = (across[j] * mask).astype(BF).astype(F32)
        if extent < 16:
            a = jnp.concatenate([a] * (16 // extent), 0)
        across_ref[j, :, :] = a.astype(BF)
    for i in range(POOL):
        d = down[i]
        if extent < 16:
            half = lax.broadcasted_iota(jnp.int32, (16, LANES), 0) < extent
            for q in range(extent // 2):
                top = jnp.broadcast_to(d[2 * q : 2 * q + 1], (16, LANES))
                low = jnp.broadcast_to(d[2 * q + 1 : 2 * q + 2], (16, LANES))
                down_ref[i, q] = jnp.where(half, top, low).astype(BF)
        else:
            for h in range(extent):
                down_ref[i, h] = jnp.broadcast_to(d[h : h + 1], (16, LANES)).astype(BF)


def kernel_row(k_ref, across_ref, down_ref, i, extent):
    wide = max(extent, 16)
    tiles = extent if extent >= 16 else extent // 2

    def body(q, c):
        d = down_ref[i, q]
        for j in range(POOL):
            for v in range(wide // 16):
                k_ref[pl.ds(pl.multiple_of(q * wide + v * 16, 16), 16), j * LANES : (j + 1) * LANES] = (
                    across_ref[j, v * 16 : (v + 1) * 16, :] * d
                )
        return c

    lax.fori_loop(0, tiles, body, 0, unroll=min(tiles, 8))


def sort_tables(table):
    n = table.shape[1]
    level = table[9:10]
    which = lax.broadcasted_iota(jnp.int32, (8, n), 0).astype(F32)
    onehot = (level == which).astype(F32)
    before = (
        lax.broadcasted_iota(jnp.int32, (n, n), 0) < lax.broadcasted_iota(jnp.int32, (n, n), 1)
    ).astype(BF)
    earlier = jnp.dot(onehot.astype(BF), before, preferred_element_type=F32)
    lower = (which < level).astype(F32) * 1.0
    counts = jnp.sum(onehot, axis=1, keepdims=True)
    rank = jnp.sum(onehot * earlier + lower * counts, axis=0, keepdims=True)
    return rank


def permute(table, rank):
    n = table.shape[1]
    place = lax.broadcasted_iota(jnp.int32, (n, n), 0).astype(F32)
    q = (rank == place).astype(F32)
    return lax.dot_general(
        table, q, (((1,), (1,)), ((), ())), precision=lax.Precision.HIGHEST, preferred_element_type=F32
    )


def forward_kernel(table_ref, p2, p3, p4, p5, out_ref, sorted_ref, acc, acr, dwn, kbuf, *, channels):
    pyr = (p2, p3, p4, p5)
    tile = pl.program_id(0)

    @pl.when(tile == 0)
    def _():
        table = table_ref[...]
        rank = sort_tables(table)
        full = permute(table, rank)
        sorted_ref[0:16, :] = full
        sorted_ref[16:24, :] = jnp.broadcast_to(rank, (8, table.shape[1]))

    rows = sorted_ref[0:16, pl.ds(pl.multiple_of(tile * LANES, LANES), LANES)]
    acc[...] = jnp.zeros_like(acc)
    first = rows[8:9] == 0.0
    cells = POOL * POOL
    for level in range(4):
        extent = SIDE // 2**level
        size = extent * extent
        here = jnp.sum((rows[9:10] == float(level)).astype(F32)) > 0.0

        @pl.when(here)
        def _():
            wide = max(extent, 16)
            a_ref = acr.at[:, 0:wide, :]
            write_tables(a_ref, dwn, rows, extent, level)
            k_ref = kbuf.at[0:size, :]

            def row(i, c):
                kernel_row(k_ref, a_ref, dwn, i, extent)
                got = jnp.dot(pyr[level][...], k_ref[...], preferred_element_type=F32)
                sel = jnp.where(
                    jnp.concatenate([first] * POOL, 1), got[:channels], got[channels:]
                )
                for j in range(POOL):
                    at = pl.ds(i * POOL + j, channels, stride=cells)
                    acc[at, :] = acc[at, :] + sel[:, j * LANES : (j + 1) * LANES]
                return c

            lax.fori_loop(0, POOL, row, 0)

    out_ref[...] = acc[...].astype(BF)


def pool_forward(table, maps, channels):
    n = table.shape[1]
    flat = channels * POOL * POOL
    full = lambda a: pl.BlockSpec(a.shape, lambda t: (0,) * a.ndim)
    return pl.pallas_call(
        functools.partial(forward_kernel, channels=channels),
        grid=(n // LANES,),
        in_specs=[full(table)] + [full(m) for m in maps],
        out_specs=[
            pl.BlockSpec((flat, LANES), lambda t: (0, t)),
            pl.BlockSpec((24, n), lambda t: (0, 0)),
        ],
        out_shape=[
            jax.ShapeDtypeStruct((flat, n), BF),
            jax.ShapeDtypeStruct((24, n), F32),
        ],
        scratch_shapes=[
            pltpu.VMEM((flat, LANES), F32),
            pltpu.VMEM((POOL, SIDE, LANES), BF),
            pltpu.VMEM((POOL, SIDE, 16, LANES), BF),
            pltpu.VMEM((SIDE * SIDE, POOL * LANES), BF),
        ],
        compiler_params=pltpu.CompilerParams(vmem_limit_bytes=VM),
        name="pool_forward",
    )(table, *maps)


def backward_kernel(sorted_ref, gp_ref, o2, o3, o4, o5, g32, acr, dwn, kbuf, gbuf, *, channels):
    outs = (o2, o3, o4, o5)
    tile = pl.program_id(0)

    @pl.when(tile == 0)
    def _():
        for o in outs:
            o[...] = jnp.zeros_like(o)

    rows = sorted_ref[0:16, pl.ds(pl.multiple_of(tile * LANES, LANES), LANES)]
    g32[...] = gp_ref[...].astype(F32) * (1.0 / 3.0)
    first = rows[8:9] == 0.0
    cells = POOL * POOL
    for level in range(4):
        extent = SIDE // 2**level
        size = extent * extent
        here = jnp.sum((rows[9:10] == float(level)).astype(F32)) > 0.0

        @pl.when(here)
        def _():
            wide = max(extent, 16)
            a_ref = acr.at[:, 0:wide, :]
            write_tables(a_ref, dwn, rows, extent, level)
            k_ref = kbuf.at[0:size, :]

            def row(i, c):
                kernel_row(k_ref, a_ref, dwn, i, extent)
                for j in range(POOL):
                    g = g32[pl.ds(i * POOL + j, channels, stride=cells), :]
                    gbuf[0:channels, j * LANES : (j + 1) * LANES] = jnp.where(first, g, 0.0).astype(BF)
                    gbuf[channels:, j * LANES : (j + 1) * LANES] = jnp.where(first, 0.0, g).astype(BF)
                outs[level][...] += lax.dot_general(
                    gbuf[...], k_ref[...], (((1,), (1,)), ((), ())), preferred_element_type=F32
                )
                return c

            lax.fori_loop(0, POOL, row, 0)


def pool_backward(sorted_table, gp, channels):
    n = sorted_table.shape[1]
    flat = channels * POOL * POOL
    sizes = [(SIDE // 2**l) ** 2 for l in range(4)]
    return pl.pallas_call(
        functools.partial(backward_kernel, channels=channels),
        grid=(n // LANES,),
        in_specs=[
            pl.BlockSpec(sorted_table.shape, lambda t: (0, 0)),
            pl.BlockSpec((flat, LANES), lambda t: (0, t)),
        ],
        out_specs=[pl.BlockSpec((2 * channels, s), lambda t: (0, 0)) for s in sizes],
        out_shape=[jax.ShapeDtypeStruct((2 * channels, s), F32) for s in sizes],
        scratch_shapes=[
            pltpu.VMEM((flat, LANES), F32),
            pltpu.VMEM((POOL, SIDE, LANES), BF),
            pltpu.VMEM((POOL, SIDE, 16, LANES), BF),
            pltpu.VMEM((SIDE * SIDE, POOL * LANES), BF),
            pltpu.VMEM((2 * channels, POOL * LANES), BF),
        ],
        compiler_params=pltpu.CompilerParams(vmem_limit_bytes=VM),
        name="pool_backward",
    )(sorted_table, gp)


def decode_boxes(corners, deltas):
    widths = corners[2] - corners[0]
    heights = corners[3] - corners[1]
    centre_x = corners[0] + 0.5 * widths
    centre_y = corners[1] + 0.5 * heights
    moved_x = deltas[:, 0] / 10.0 * widths + centre_x
    moved_y = deltas[:, 1] / 10.0 * heights + centre_y
    new_width = jnp.exp(deltas[:, 2] / 5.0) * widths
    new_height = jnp.exp(deltas[:, 3] / 5.0) * heights
    return jnp.stack(
        [
            moved_x - 0.5 * new_width,
            moved_y - 0.5 * new_height,
            moved_x + 0.5 * new_width,
            moved_y + 0.5 * new_height,
        ]
    )


def column_sums(matrix):
    return jnp.sum(matrix.astype(jnp.float32), axis=0)


def transposed_product(left_rows, right_rows):
    return lax.dot_general(
        left_rows, right_rows, (((0,), (0,)), ((), ())), preferred_element_type=jnp.float32
    )


def product_with_transpose(left_rows, right_rows):
    return lax.dot_general(
        left_rows, right_rows, (((1,), (1,)), ((), ())), preferred_element_type=jnp.float32
    )


def head_pass(
    summed,
    first_bias,
    second_weight,
    second_bias,
    class_weight,
    class_bias,
    box_weight,
    box_bias,
    label_rows,
    target_rows,
    corner_rows,
    norm_count,
):
    pre_one = summed + first_bias.astype(jnp.float32)
    act_one, gelu_one = jax.vjp(smooth_unit, pre_one)
    act_one = act_one.astype(jnp.bfloat16)
    pre_two = jnp.dot(
        act_one, second_weight, preferred_element_type=jnp.float32
    ) + second_bias.astype(jnp.float32)
    act_two, gelu_two = jax.vjp(smooth_unit, pre_two)
    act_two = act_two.astype(jnp.bfloat16)
    logits = jnp.dot(act_two, class_weight, preferred_element_type=jnp.float32) + class_bias.astype(
        jnp.float32
    )
    deltas = jnp.dot(act_two, box_weight, preferred_element_type=jnp.float32) + box_bias.astype(
        jnp.float32
    )
    classes = logits.shape[1]
    row_max = jnp.max(logits, axis=1, keepdims=True)
    exponent = jnp.exp(logits - row_max)
    row_total = jnp.sum(exponent, axis=1, keepdims=True)
    onehot = (label_rows[:, None] == jnp.arange(classes, dtype=jnp.int32)[None, :]).astype(
        jnp.float32
    )
    class_part = (
        jnp.sum(row_max[:, 0] + jnp.log(row_total[:, 0]) - jnp.sum(logits * onehot, axis=1))
        / norm_count
    )
    foreground = (label_rows < classes - 1).astype(jnp.float32)[:, None]
    residue = deltas - target_rows.T
    magnitude = jnp.abs(residue)
    huber = jnp.where(magnitude < 1.0, 0.5 * residue * residue, magnitude - 0.5)
    box_part = jnp.sum(foreground * huber) / norm_count
    grad_logits = ((exponent / row_total - onehot) / norm_count).astype(jnp.bfloat16)
    grad_deltas = (foreground * jnp.clip(residue, -1.0, 1.0) / norm_count).astype(jnp.bfloat16)
    grad_weight_class = transposed_product(act_two, grad_logits)
    grad_bias_class = column_sums(grad_logits)
    grad_weight_box = transposed_product(act_two, grad_deltas)
    grad_bias_box = column_sums(grad_deltas)
    grad_act_two = product_with_transpose(grad_logits, class_weight) + product_with_transpose(
        grad_deltas, box_weight
    )
    grad_pre_two = gelu_two(grad_act_two)[0].astype(jnp.bfloat16)
    grad_weight_two = transposed_product(act_one, grad_pre_two)
    grad_bias_two = column_sums(grad_pre_two)
    grad_act_one = product_with_transpose(grad_pre_two, second_weight)
    grad_pre_one = gelu_one(grad_act_one)[0].astype(jnp.bfloat16)
    grad_bias_one = column_sums(grad_pre_one)
    decoded = decode_boxes(corner_rows, deltas)
    small_grads = (
        grad_bias_one,
        grad_weight_two,
        grad_bias_two,
        grad_weight_class,
        grad_bias_class,
        grad_weight_box,
        grad_bias_box,
        class_part,
        box_part,
    )
    return (grad_pre_one, small_grads, decoded)


def smooth_unit(values):
    return jax.nn.gelu(values, approximate=False)


def on_device(
    pyramid_two,
    pyramid_three,
    pyramid_four,
    pyramid_five,
    proposals,
    image_index,
    levels,
    labels,
    targets,
    first_weight,
    first_bias,
    second_weight,
    second_bias,
    class_weight,
    class_bias,
    box_weight,
    box_bias,
):
    features = (pyramid_two, pyramid_three, pyramid_four, pyramid_five)
    images_here, channels_here = (pyramid_two.shape[0], pyramid_two.shape[1])
    regions_here = proposals.shape[1]
    local_image = image_index - lax.axis_index("roi") * images_here
    maps = [f.reshape(images_here * channels_here, -1) for f in features]
    table = jnp.concatenate(
        [
            proposals,
            targets,
            local_image[None].astype(F32),
            levels[None].astype(F32),
            labels[None].astype(F32),
            jnp.zeros((5, regions_here), F32),
        ]
    )
    pooled, ordered = pool_forward(table, maps, channels_here)
    norm_count = float(regions_here * lax.axis_size("roi"))
    partial = lax.dot_general(
        pooled, first_weight, (((0,), (0,)), ((), ())), preferred_element_type=F32
    )
    if lax.axis_size("ch") == 2:
        partial = partial.astype(BF)
        other = lax.ppermute(partial, "ch", [(0, 1), (1, 0)])
        summed = partial.astype(F32) + other.astype(F32)
    else:
        summed = lax.psum(partial, "ch")
    grad_pre_one, small_grads, decoded = head_pass(
        summed,
        first_bias,
        second_weight,
        second_bias,
        class_weight,
        class_bias,
        box_weight,
        box_bias,
        ordered[10].astype(jnp.int32),
        ordered[4:8],
        ordered[0:4],
        norm_count,
    )
    grad_weight_one = lax.dot_general(
        pooled, grad_pre_one, (((1,), (0,)), ((), ())), preferred_element_type=F32
    ).astype(BF)
    grad_pooled = lax.dot_general(
        first_weight, grad_pre_one, (((1,), (1,)), ((), ())), preferred_element_type=F32
    ).astype(BF)
    grad_weight_one, grad_weight_two = lax.psum((grad_weight_one, small_grads[1].astype(BF)), "roi")
    small = lax.psum(small_grads[0:1] + small_grads[2:], "roi")
    grad_bias_one, grad_bias_two, grad_weight_class, grad_bias_class, grad_weight_box, grad_bias_box, class_loss, box_loss = small
    rank = ordered[16]
    place = jnp.arange(regions_here, dtype=F32)
    back = (place[:, None] == rank[None, :]).astype(F32)
    decoded = jnp.dot(decoded, back, precision=lax.Precision.HIGHEST)
    share_rows = regions_here // lax.axis_size("ch")
    decoded = lax.dynamic_slice_in_dim(decoded, lax.axis_index("ch") * share_rows, share_rows, 1)
    map_grads = pool_backward(ordered, grad_pooled, channels_here)
    pyramid_grads = [g.reshape(f.shape) for g, f in zip(map_grads, features)]
    return (
        class_loss,
        box_loss,
        decoded,
        grad_weight_one.astype(F32),
        grad_bias_one,
        grad_weight_two.astype(F32),
        grad_bias_two,
        grad_weight_class,
        grad_bias_class,
        grad_weight_box,
        grad_bias_box,
        pyramid_grads[0],
        pyramid_grads[1],
        pyramid_grads[2],
        pyramid_grads[3],
    )


def solution(mesh):
    return jax.shard_map(
        on_device,
        mesh=mesh,
        in_specs=(
            P("roi", "ch", None),
            P("roi", "ch", None),
            P("roi", "ch", None),
            P("roi", "ch", None),
            P(None, "roi"),
            P("roi"),
            P("roi"),
            P("roi"),
            P(None, "roi"),
            P("ch", None),
            P(),
            P(),
            P(),
            P(),
            P(),
            P(),
            P(),
        ),
        out_specs=(
            P(),
            P(),
            P(None, ("roi", "ch")),
            P("ch", None),
            P(),
            P(),
            P(),
            P(),
            P(),
            P(),
            P(),
            P("roi", "ch", None),
            P("roi", "ch", None),
            P("roi", "ch", None),
            P("roi", "ch", None),
        ),
        check_vma=False,
    )
```

```python
import functools
import jax, jax.numpy as jnp
from jax import lax
from jax.sharding import PartitionSpec as P
from jax.experimental import pallas as pl
from jax.experimental.pallas import tpu as pltpu

POOL = 7
SAMPLES = 2
SIDE = 64
LANES = 128
BF = jnp.bfloat16
F32 = jnp.float32
VM = 60 * 2**20


def spread(low, high, extent):
    anchor = low * extent - 0.5
    stride = (high - low) * extent / POOL
    places = lax.broadcasted_iota(jnp.int32, (extent, LANES), 0).astype(F32)
    out = []
    for col in range(POOL):
        total = None
        for s in range(SAMPLES):
            at = jnp.clip(anchor + (col + (s + 0.5) / SAMPLES) * stride, 0.0, extent - 1.0)
            term = jnp.maximum(0.0, 1.0 - jnp.abs(at - places))
            total = term if total is None else total + term
        out.append(total / SAMPLES)
    return out


def write_tables(across_ref, down_ref, rows, extent, level):
    x1, y1, x2, y2 = (rows[k : k + 1] for k in range(4, 8))
    mask = (rows[9:10] == float(level)).astype(F32)
    across = spread(x1, x2, extent)
    down = spread(y1, y2, extent)
    for j in range(POOL):
        a = (across[j] * mask).astype(BF).astype(F32)
        if extent < 16:
            a = jnp.concatenate([a] * (16 // extent), 0)
        across_ref[j, :, :] = a.astype(BF)
    for i in range(POOL):
        d = down[i]
        if extent < 16:
            half = lax.broadcasted_iota(jnp.int32, (16, LANES), 0) < extent
            for q in range(extent // 2):
                top = jnp.broadcast_to(d[2 * q : 2 * q + 1], (16, LANES))
                low = jnp.broadcast_to(d[2 * q + 1 : 2 * q + 2], (16, LANES))
                down_ref[i, q] = jnp.where(half, top, low).astype(BF)
        else:
            for h in range(extent):
                down_ref[i, h] = jnp.broadcast_to(d[h : h + 1], (16, LANES)).astype(BF)


def kernel_row(k_ref, across_ref, down_ref, i, extent):
    wide = max(extent, 16)
    tiles = extent * extent // wide
    down = down_ref[i, 0:tiles].reshape(tiles, 1, 16, LANES)
    for j in range(POOL):
        across = across_ref[j, 0:wide, :].reshape(1, wide // 16, 16, LANES)
        k_ref[0 : extent * extent, j * LANES : (j + 1) * LANES] = (across * down).reshape(
            extent * extent, LANES
        )


def over_rows(k_refs, make, use):
    first, second = k_refs
    make(first, 0)

    def pair(p, c):
        make(second, 2 * p + 1)
        use(first, 2 * p)
        make(first, 2 * p + 2)
        use(second, 2 * p + 1)
        return c

    lax.fori_loop(0, POOL // 2, pair, 0)
    use(first, POOL - 1)


def sort_tables(table):
    n = table.shape[1]
    level = table[9:10]
    which = lax.broadcasted_iota(jnp.int32, (8, n), 0).astype(F32)
    onehot = (level == which).astype(F32)
    before = (
        lax.broadcasted_iota(jnp.int32, (n, n), 0) < lax.broadcasted_iota(jnp.int32, (n, n), 1)
    ).astype(BF)
    earlier = jnp.dot(onehot.astype(BF), before, preferred_element_type=F32)
    lower = (which < level).astype(F32) * 1.0
    counts = jnp.sum(onehot, axis=1, keepdims=True)
    rank = jnp.sum(onehot * earlier + lower * counts, axis=0, keepdims=True)
    return rank


def permute(table, rank):
    n = table.shape[1]
    place = lax.broadcasted_iota(jnp.int32, (n, n), 0).astype(F32)
    q = (rank == place).astype(F32)
    return lax.dot_general(
        table, q, (((1,), (1,)), ((), ())), precision=lax.Precision.HIGHEST, preferred_element_type=F32
    )


def forward_kernel(base_ref, boxes_ref, targets_ref, image_ref, level_ref, label_ref, p2, p3, p4, p5, out_ref, sorted_ref, acc, acr, dwn, kone, ktwo, *, channels):
    pyr = (p2, p3, p4, p5)
    tile = pl.program_id(0)

    @pl.when(tile == 0)
    def _():
        count = boxes_ref.shape[1]
        table = jnp.concatenate(
            [
                targets_ref[...],
                boxes_ref[...],
                (image_ref[...] - base_ref[0]).astype(F32),
                level_ref[...].astype(F32),
                label_ref[...].astype(F32),
                jnp.zeros((5, count), F32),
            ]
        )
        rank = sort_tables(table)
        full = permute(table, rank)
        sorted_ref[0:16, :] = full
        sorted_ref[16:24, :] = jnp.broadcast_to(rank, (8, count))

    rows = sorted_ref[0:16, pl.ds(pl.multiple_of(tile * LANES, LANES), LANES)]
    acc[...] = jnp.zeros_like(acc)
    first = rows[8:9] == 0.0
    cells = POOL * POOL
    for level in range(4):
        extent = SIDE // 2**level
        size = extent * extent
        here = jnp.sum((rows[9:10] == float(level)).astype(F32)) > 0.0

        @pl.when(here)
        def _():
            wide = max(extent, 16)
            a_ref = acr.at[:, 0:wide, :]
            write_tables(a_ref, dwn, rows, extent, level)

            def make(k_ref, i):
                kernel_row(k_ref, a_ref, dwn, i, extent)

            def use(k_ref, i):
                got = jnp.dot(pyr[level][...], k_ref[0:size, :], preferred_element_type=F32)
                sel = jnp.where(
                    jnp.concatenate([first] * POOL, 1), got[:channels], got[channels:]
                )
                for j in range(POOL):
                    at = pl.ds(i * POOL + j, channels, stride=cells)
                    acc[at, :] = acc[at, :] + sel[:, j * LANES : (j + 1) * LANES]

            over_rows((kone, ktwo), make, use)

    out_ref[...] = acc[...].astype(BF)


def pool_forward(base, boxes, targets, image, level, label, maps, channels):
    n = boxes.shape[1]
    rows = (boxes, targets, image, level, label)
    flat = channels * POOL * POOL
    full = lambda a: pl.BlockSpec(a.shape, lambda t: (0,) * a.ndim)
    return pl.pallas_call(
        functools.partial(forward_kernel, channels=channels),
        grid=(n // LANES,),
        in_specs=[pl.BlockSpec(memory_space=pltpu.SMEM)] + [full(a) for a in rows] + [full(m) for m in maps],
        out_specs=[
            pl.BlockSpec((flat, LANES), lambda t: (0, t)),
            pl.BlockSpec((24, n), lambda t: (0, 0)),
        ],
        out_shape=[
            jax.ShapeDtypeStruct((flat, n), BF),
            jax.ShapeDtypeStruct((24, n), F32),
        ],
        scratch_shapes=[
            pltpu.VMEM((flat, LANES), F32),
            pltpu.VMEM((POOL, SIDE, LANES), BF),
            pltpu.VMEM((POOL, SIDE, 16, LANES), BF),
            pltpu.VMEM((SIDE * SIDE, POOL * LANES), BF),
            pltpu.VMEM((SIDE * SIDE, POOL * LANES), BF),
        ],
        compiler_params=pltpu.CompilerParams(vmem_limit_bytes=VM),
        cost_estimate=pl.CostEstimate(flops=40 * 10**9, bytes_accessed=10**7, transcendentals=0),
        name="pool_forward",
    )(base, *rows, *maps)


def backward_kernel(sorted_ref, gp_ref, o2, o3, o4, o5, g32, acr, dwn, kone, ktwo, gbuf, *, channels):
    outs = (o2, o3, o4, o5)
    tile = pl.program_id(0)

    @pl.when(tile == 0)
    def _():
        for o in outs:
            o[...] = jnp.zeros_like(o)

    rows = sorted_ref[0:16, pl.ds(pl.multiple_of(tile * LANES, LANES), LANES)]
    g32[...] = gp_ref[...].astype(F32) * (1.0 / 3.0)
    first = rows[8:9] == 0.0
    cells = POOL * POOL
    for level in range(4):
        extent = SIDE // 2**level
        size = extent * extent
        here = jnp.sum((rows[9:10] == float(level)).astype(F32)) > 0.0

        @pl.when(here)
        def _():
            wide = max(extent, 16)
            a_ref = acr.at[:, 0:wide, :]
            write_tables(a_ref, dwn, rows, extent, level)

            def make(k_ref, i):
                kernel_row(k_ref, a_ref, dwn, i, extent)

            def use(k_ref, i):
                for j in range(POOL):
                    g = g32[pl.ds(i * POOL + j, channels, stride=cells), :]
                    gbuf[0:channels, j * LANES : (j + 1) * LANES] = jnp.where(first, g, 0.0).astype(BF)
                    gbuf[channels:, j * LANES : (j + 1) * LANES] = jnp.where(first, 0.0, g).astype(BF)
                outs[level][...] += lax.dot_general(
                    gbuf[...], k_ref[0:size, :], (((1,), (1,)), ((), ())), preferred_element_type=F32
                )

            over_rows((kone, ktwo), make, use)


def pool_backward(sorted_table, gp, channels):
    n = sorted_table.shape[1]
    flat = channels * POOL * POOL
    sizes = [(SIDE // 2**l) ** 2 for l in range(4)]
    return pl.pallas_call(
        functools.partial(backward_kernel, channels=channels),
        grid=(n // LANES,),
        in_specs=[
            pl.BlockSpec(sorted_table.shape, lambda t: (0, 0)),
            pl.BlockSpec((flat, LANES), lambda t: (0, t)),
        ],
        out_specs=[pl.BlockSpec((2 * channels, s), lambda t: (0, 0)) for s in sizes],
        out_shape=[jax.ShapeDtypeStruct((2 * channels, s), F32) for s in sizes],
        scratch_shapes=[
            pltpu.VMEM((flat, LANES), F32),
            pltpu.VMEM((POOL, SIDE, LANES), BF),
            pltpu.VMEM((POOL, SIDE, 16, LANES), BF),
            pltpu.VMEM((SIDE * SIDE, POOL * LANES), BF),
            pltpu.VMEM((SIDE * SIDE, POOL * LANES), BF),
            pltpu.VMEM((2 * channels, POOL * LANES), BF),
        ],
        compiler_params=pltpu.CompilerParams(vmem_limit_bytes=VM),
        cost_estimate=pl.CostEstimate(flops=40 * 10**9, bytes_accessed=10**7, transcendentals=0),
        name="pool_backward",
    )(sorted_table, gp)


BOX = 96
ROOT = 0.7071067811865476
DENSITY = 0.3989422804014327
STRIP = 16


def unit_and_slope(x):
    below = 0.5 + 0.5 * lax.erf(x * ROOT)
    return x * below, below + x * jnp.exp(-0.5 * x * x) * DENSITY


def strips(rows, work, carry):
    def step(k, c):
        return work(pl.ds(pl.multiple_of(k * STRIP, STRIP), STRIP), c)

    return lax.fori_loop(0, rows // STRIP, step, carry)


def head_kernel(
    part_ref,
    ordered_ref,
    own_ref,
    other_ref,
    bias_one,
    weight_two,
    bias_two,
    weight_out,
    bias_out,
    grad_one,
    grad_two_weight,
    small,
    last,
    decoded_ref,
    act_one,
    act_two,
    grad_two,
    slope_one,
    slope_two,
    wide,
    *,
    classes,
    norm,
):
    rows, hidden = own_ref.shape
    lanes = weight_out.shape[1]

    def one(at, c):
        x = own_ref[at, :].astype(F32) + other_ref[at, :].astype(F32) + bias_one[...]
        act, slope = unit_and_slope(x)
        act_one[at, :] = act.astype(BF)
        slope_one[at, :] = slope
        return c

    strips(rows, one, 0)
    wide[...] = jnp.dot(act_one[...], weight_two[...], preferred_element_type=F32)

    def two(at, c):
        act, slope = unit_and_slope(wide[at, :] + bias_two[...])
        act_two[at, :] = act.astype(BF)
        slope_two[at, :] = slope
        return c

    strips(rows, two, 0)
    out = jnp.dot(act_two[...], weight_out[...], preferred_element_type=F32) + bias_out[...]
    ordered = ordered_ref[...]
    aux = jnp.concatenate(
        [
            jnp.zeros((BOX - 8, rows), F32),
            ordered[8:16],
            ordered[0:8],
            jnp.zeros((lanes - BOX - 8, rows), F32),
        ]
    ).T
    lane = lax.broadcasted_iota(jnp.int32, (rows, lanes), 1)
    is_class = lane < classes
    is_box = (lane >= BOX) & (lane < BOX + 4)
    label = aux[:, BOX - 6 : BOX - 5]
    hit = (lane.astype(F32) == label).astype(F32)
    fore = (label < classes - 1.0).astype(F32)
    scores = jnp.where(is_class, out, -3.0e38)
    top = jnp.max(scores, axis=1, keepdims=True)
    powers = jnp.where(is_class, jnp.exp(scores - top), 0.0)
    total = jnp.sum(powers, axis=1, keepdims=True)
    chosen = jnp.sum(jnp.where(is_class, out * hit, 0.0), axis=1, keepdims=True)
    class_loss = jnp.sum(top + jnp.log(total) - chosen, axis=0, keepdims=True) / norm
    residue = out - aux
    size = jnp.abs(residue)
    huber = jnp.where(size < 1.0, 0.5 * residue * residue, size - 0.5)
    huber = jnp.sum(jnp.where(is_box, huber, 0.0), axis=1, keepdims=True) * fore
    box_loss = jnp.sum(huber, axis=0, keepdims=True) / norm
    grad_out = jnp.where(
        is_class,
        (powers / total - hit) / norm,
        jnp.where(is_box, fore * jnp.clip(residue, -1.0, 1.0) / norm, 0.0),
    ).astype(BF)
    bias_sums = jnp.sum(grad_out.astype(F32), axis=0, keepdims=True)
    last[...] = jnp.concatenate(
        [
            bias_sums,
            jnp.broadcast_to(class_loss, (1, lanes)),
            jnp.broadcast_to(box_loss, (1, lanes)),
            jnp.zeros((5, lanes), F32),
        ]
    )
    moves = out.T[BOX : BOX + 4]
    x1, y1, x2, y2 = (ordered[k : k + 1] for k in range(4, 8))
    width, height = x2 - x1, y2 - y1
    px = moves[0:1] / 10.0 * width + (x1 + 0.5 * width)
    py = moves[1:2] / 10.0 * height + (y1 + 0.5 * height)
    half_w = 0.5 * (jnp.exp(moves[2:3] / 5.0) * width)
    half_h = 0.5 * (jnp.exp(moves[3:4] / 5.0) * height)
    boxes = jnp.concatenate(
        [px - half_w, py - half_h, px + half_w, py + half_h, jnp.zeros((4, rows), F32)]
    )
    place = lax.broadcasted_iota(jnp.int32, (rows, rows), 0).astype(F32)
    back = (ordered_ref[16:17, :] == place).astype(F32)
    decoded_ref[...] = jnp.dot(
        boxes, back, precision=lax.Precision.HIGHEST, preferred_element_type=F32
    )
    wide[...] = lax.dot_general(
        grad_out, weight_out[...], (((1,), (1,)), ((), ())), preferred_element_type=F32
    )

    def three(at, c):
        g = (wide[at, :] * slope_two[at, :]).astype(BF)
        grad_two[at, :] = g
        g = g.astype(F32)
        return c + g[0:8] + g[8:16]

    bias_two_sum = strips(rows, three, jnp.zeros((8, hidden), F32))
    wide[...] = lax.dot_general(
        grad_two[...], weight_two[...], (((1,), (1,)), ((), ())), preferred_element_type=F32
    )

    def four(at, c):
        g = (wide[at, :] * slope_one[at, :]).astype(BF)
        grad_one[at, :] = g
        g = g.astype(F32)
        return c + g[0:8] + g[8:16]

    bias_one_sum = strips(rows, four, jnp.zeros((8, hidden), F32))
    part = grad_two_weight.shape[0]
    columns = pl.ds(pl.multiple_of(part_ref[0] * part, part), part)
    grad_two_weight[...] = lax.dot_general(
        act_one[:, columns], grad_two[...], (((0,), (0,)), ((), ())), preferred_element_type=F32
    ).astype(BF)
    products = lax.dot_general(
        grad_out, act_two[...], (((0,), (0,)), ((), ())), preferred_element_type=F32
    )
    sums = jnp.concatenate(
        [
            jnp.sum(bias_one_sum, axis=0, keepdims=True),
            jnp.sum(bias_two_sum, axis=0, keepdims=True),
            jnp.zeros((lanes - BOX - 10, hidden), F32),
        ]
    )
    small[...] = jnp.concatenate([products[: BOX + 8], sums]).astype(BF)


def head_pass(
    part, parts, ordered, own, other, bias_one, weight_two, bias_two, weight_out, bias_out, classes, norm
):
    rows, hidden = own.shape
    lanes = weight_out.shape[1]
    whole = pl.BlockSpec(memory_space=pltpu.VMEM)
    return pl.pallas_call(
        functools.partial(head_kernel, classes=classes, norm=norm),
        in_specs=[pl.BlockSpec(memory_space=pltpu.SMEM)] + [whole] * 8,
        out_specs=[whole] * 5,
        out_shape=[
            jax.ShapeDtypeStruct((rows, hidden), BF),
            jax.ShapeDtypeStruct((hidden // parts, hidden), BF),
            jax.ShapeDtypeStruct((lanes, hidden), BF),
            jax.ShapeDtypeStruct((8, lanes), F32),
            jax.ShapeDtypeStruct((8, rows), F32),
        ],
        scratch_shapes=[pltpu.VMEM((rows, hidden), BF)] * 3 + [pltpu.VMEM((rows, hidden), F32)] * 3,
        compiler_params=pltpu.CompilerParams(vmem_limit_bytes=VM),
        cost_estimate=pl.CostEstimate(
            flops=6 * rows * hidden * hidden, bytes_accessed=8 * rows * hidden, transcendentals=0
        ),
        name="head",
    )(part, ordered, own, other, bias_one, weight_two, bias_two, weight_out, bias_out)


def partners(stride):
    return [(k, k ^ stride) for k in range(lax.axis_size("roi"))]


def halve(sums, axis, stride, size):
    while size > 1:
        mine = (lax.axis_index("roi") // stride) % 2
        shape = sums.shape
        split = sums.reshape(shape[:axis] + (size // 2, 2) + shape[axis + 1 :])
        keep = lax.dynamic_index_in_dim(split, mine, axis + 1, False)
        send = lax.dynamic_index_in_dim(split, 1 - mine, axis + 1, False)
        come = lax.ppermute(send, "roi", partners(stride))
        sums = (keep.astype(F32) + come.astype(F32)).astype(BF)
        stride, size = 2 * stride, size // 2
    return lax.squeeze(sums, (axis,))


def add_up_everywhere(values):
    stride = 1
    while stride < lax.axis_size("roi"):
        values = values + lax.ppermute(values, "roi", partners(stride))
        stride *= 2
    return values


def row_parts(rows):
    unit = 8 if rows % 8 == 0 else 1
    units = rows // unit
    last = max(1, units // 4)
    first = (units - last) // 2
    return (first * unit, (units - last - first) * unit, last * unit)


def spread_out(mine):
    stride, axis, shape = lax.axis_size("roi") // 2, 0, mine.shape
    while stride:
        low = (lax.axis_index("roi") // stride) % 2 == 0
        come = lax.ppermute(mine, "roi", partners(stride))
        mine = jnp.stack([jnp.where(low, mine, come), jnp.where(low, come, mine)], axis)
        stride, axis = stride // 2, axis + 1
    return mine.reshape(-1, shape[-1])


def on_device(
    pyramid_two,
    pyramid_three,
    pyramid_four,
    pyramid_five,
    proposals,
    image_index,
    levels,
    labels,
    targets,
    first_weight,
    first_bias,
    second_weight,
    second_bias,
    class_weight,
    class_bias,
    box_weight,
    box_bias,
):
    features = (pyramid_two, pyramid_three, pyramid_four, pyramid_five)
    images_here, channels_here = (pyramid_two.shape[0], pyramid_two.shape[1])
    regions_here = proposals.shape[1]
    ways, groups = lax.axis_size("roi"), lax.axis_size("ch")
    outer, inner = 4, ways // 8
    flat, hidden = first_weight.shape
    classes = class_weight.shape[1]
    share = flat // ways
    core = lax.axis_index("roi") % 2
    group = lax.axis_index("ch")
    maps = [f.reshape(images_here * channels_here, -1) for f in features]
    base = jnp.reshape(lax.axis_index("roi") * images_here, (1,)).astype(jnp.int32)
    pooled, ordered = pool_forward(
        base, proposals, targets, image_index[None], levels[None], labels[None], maps, channels_here
    )
    partial = lax.dot_general(
        pooled, first_weight, (((0,), (0,)), ((), ())), preferred_element_type=F32
    )
    if groups == 2:
        partial = partial.astype(BF)
        other = lax.ppermute(partial, "ch", [(0, 1), (1, 0)])
    else:
        partial = lax.psum(partial, "ch")
        other = jnp.zeros(partial.shape, BF)
    by_core = pooled.reshape(ways // 2, 2, share, regions_here)
    mine = lax.dynamic_index_in_dim(by_core, core, 1, False)
    theirs = lax.ppermute(lax.dynamic_index_in_dim(by_core, 1 - core, 1, False), "roi", partners(1))
    both = jnp.concatenate([mine, theirs], 2)
    gap = jnp.zeros((hidden, BOX - classes), BF)
    tail = jnp.zeros((hidden, 128 - BOX - 4), BF)
    weight_out = jnp.concatenate([class_weight, gap, box_weight, tail], 1)
    bias_out = jnp.concatenate([class_bias, gap[0], box_bias, tail[0]]).astype(F32)[None]
    grad_pre_one, grad_two, small, last, decoded = head_pass(
        jnp.reshape(group, (1,)).astype(jnp.int32),
        groups,
        ordered,
        partial,
        other,
        first_bias.astype(F32)[None],
        second_weight,
        second_bias.astype(F32)[None],
        weight_out,
        bias_out,
        classes,
        float(regions_here * ways),
    )
    grad_both = jnp.concatenate([grad_pre_one, lax.ppermute(grad_pre_one, "roi", partners(1))], 0)
    extra = jnp.concatenate([grad_two, small])
    extra_share = extra.shape[0] // ways
    extra = halve(extra.reshape(ways // 2, 2, extra_share, hidden), 1, 1, 2)
    extra = extra.reshape(outer, inner, extra_share, hidden)
    parts, at = [], 0
    split = row_parts(share)
    for rows in split:
        rows_both = both[:, at : at + rows].reshape(-1, 2 * regions_here)
        part = jnp.dot(rows_both, grad_both, preferred_element_type=F32).astype(BF)
        parts.append(part.reshape(outer, inner, rows, hidden))
        at += rows
    parts[2] = jnp.concatenate([parts[2], extra], 2)
    first_sum = halve(halve(parts[0], 1, 2, inner), 0, 2 * inner, outer)
    second_sum = halve(halve(parts[1], 1, 2, inner), 0, 2 * inner, outer)
    third_sum = halve(halve(parts[2], 0, 2 * inner, outer), 0, 2, inner)
    share_sum = jnp.concatenate([first_sum, second_sum, third_sum[: split[2]]])
    grad_weight_one = lax.all_gather(share_sum, "roi", tiled=True).astype(F32)
    extra = spread_out(third_sum[split[2] :])
    part_rows = hidden // groups
    small = extra[part_rows:].astype(F32)
    if groups == 2:
        two = extra[:part_rows]
        two_other = lax.ppermute(two, "ch", [(0, 1), (1, 0)])
        two = jnp.concatenate(
            [jnp.where(group == 0, two, two_other), jnp.where(group == 0, two_other, two)]
        )
    else:
        two = lax.all_gather(extra[:part_rows], "ch", tiled=True)
    grad_pooled = lax.dot_general(
        first_weight, grad_pre_one, (((1,), (1,)), ((), ())), preferred_element_type=F32
    ).astype(BF)
    last = add_up_everywhere(last)
    share_rows = regions_here // groups
    decoded = lax.dynamic_slice(decoded, (0, group * share_rows), (4, share_rows))
    map_grads = pool_backward(ordered, grad_pooled, channels_here)
    pyramid_grads = [g.reshape(f.shape) for g, f in zip(map_grads, features)]
    return (
        last[1, 0],
        last[2, 0],
        decoded,
        grad_weight_one,
        small[BOX + 8],
        two.astype(F32),
        small[BOX + 9],
        small[:classes].T,
        last[0, :classes],
        small[BOX : BOX + 4].T,
        last[0, BOX : BOX + 4],
        pyramid_grads[0],
        pyramid_grads[1],
        pyramid_grads[2],
        pyramid_grads[3],
    )


def solution(mesh):
    return jax.shard_map(
        on_device,
        mesh=mesh,
        in_specs=(
            P("roi", "ch", None),
            P("roi", "ch", None),
            P("roi", "ch", None),
            P("roi", "ch", None),
            P(None, "roi"),
            P("roi"),
            P("roi"),
            P("roi"),
            P(None, "roi"),
            P("ch", None),
            P(),
            P(),
            P(),
            P(),
            P(),
            P(),
            P(),
        ),
        out_specs=(
            P(),
            P(),
            P(None, ("roi", "ch")),
            P("ch", None),
            P(),
            P(),
            P(),
            P(),
            P(),
            P(),
            P(),
            P("roi", "ch", None),
            P("roi", "ch", None),
            P("roi", "ch", None),
            P("roi", "ch", None),
        ),
        check_vma=False,
    )
```

```python
import functools
import jax, jax.numpy as jnp
from jax import lax
from jax.sharding import PartitionSpec as P
from jax.experimental import pallas as pl
from jax.experimental.pallas import tpu as pltpu

POOL = 7
SAMPLES = 2
SIDE = 64
LANES = 128
FEW = 32
PACKED = 2
SHIFT = 5
BF = jnp.bfloat16
F32 = jnp.float32
VM = 60 * 2**20


def spread_one(low, high, extent, col):
    anchor = low * extent - 0.5
    stride = (high - low) * extent / POOL
    places = lax.broadcasted_iota(jnp.int32, (extent, LANES), 0).astype(F32)
    total = None
    for s in range(SAMPLES):
        at = jnp.clip(anchor + (col + (s + 0.5) / SAMPLES) * stride, 0.0, extent - 1.0)
        term = jnp.maximum(0.0, 1.0 - jnp.abs(at - places))
        total = term if total is None else total + term
    return total / SAMPLES


def spread(low, high, extent):
    return [spread_one(low, high, extent, float(col)) for col in range(POOL)]


def write_down(down_ref, rows, extent):
    down = spread(rows[5:6], rows[7:8], extent)
    for i in range(POOL):
        d = down[i]
        if extent < 16:
            half = lax.broadcasted_iota(jnp.int32, (16, LANES), 0) < extent
            for q in range(extent // 2):
                top = jnp.broadcast_to(d[2 * q : 2 * q + 1], (16, LANES))
                low = jnp.broadcast_to(d[2 * q + 1 : 2 * q + 2], (16, LANES))
                down_ref[i, q] = jnp.where(half, top, low).astype(BF)
        else:
            for h in range(extent):
                down_ref[i, h] = jnp.broadcast_to(d[h : h + 1], (16, LANES)).astype(BF)


def write_across(across_ref, index, weights, mask, extent):
    a = (weights * mask).astype(BF).astype(F32)
    if extent < 16:
        a = jnp.concatenate([a] * (16 // extent), 0)
    across_ref[index, 0 : max(extent, 16), :] = a.astype(BF)


def write_tables(across_ref, down_ref, rows, extent, level):
    mask = (rows[9:10] == float(level)).astype(F32)
    across = spread(rows[4:5], rows[6:7], extent)
    for j in range(POOL):
        write_across(across_ref, j, across[j], mask, extent)
    write_down(down_ref, rows, extent)


def pack_lanes(rows, start):
    lane = lax.broadcasted_iota(jnp.int32, rows.shape, 1)
    rolled = pltpu.roll(rows, lax.rem(LANES - start, LANES), 1)
    few = jnp.where(lane < FEW, rolled, 0.0)
    total = few
    for k in range(1, LANES // FEW):
        total = total + pltpu.roll(few, k * FEW, 1)
    return total


def write_packed_tables(across_ref, down_ref, rows, extent, count):
    lane = lax.broadcasted_iota(jnp.int32, (1, LANES), 1)
    mask = ((lane & (FEW - 1)) < count).astype(F32)
    per = LANES // FEW
    for t in range(PACKED):
        column = (lane >> SHIFT) + t * per
        across = spread_one(rows[4:5], rows[6:7], extent, column.astype(F32))
        write_across(across_ref, t, across, mask * (column < POOL).astype(F32), extent)
    write_down(down_ref, rows, extent)


def kernel_row(k_ref, across_ref, down_ref, i, extent, lane_tiles):
    wide = max(extent, 16)
    tiles = extent * extent // wide
    down = down_ref[i, 0:tiles].reshape(tiles, 1, 16, LANES)
    for j in range(lane_tiles):
        across = across_ref[j, 0:wide, :].reshape(1, wide // 16, 16, LANES)
        k_ref[0 : extent * extent, j * LANES : (j + 1) * LANES] = (across * down).reshape(
            extent * extent, LANES
        )


def over_rows(k_refs, make, use):
    first, second = k_refs
    make(first, 0)

    def pair(p, c):
        make(second, 2 * p + 1)
        use(first, 2 * p)
        make(first, 2 * p + 2)
        use(second, 2 * p + 1)
        return c

    lax.fori_loop(0, POOL // 2, pair, 0)
    use(first, POOL - 1)


def sort_tables(table):
    n = table.shape[1]
    level = table[9:10]
    which = lax.broadcasted_iota(jnp.int32, (8, n), 0).astype(F32)
    onehot = (level == which).astype(F32)
    before = (
        lax.broadcasted_iota(jnp.int32, (n, n), 0) < lax.broadcasted_iota(jnp.int32, (n, n), 1)
    ).astype(BF)
    earlier = jnp.dot(onehot.astype(BF), before, preferred_element_type=F32)
    lower = (which < level).astype(F32) * 1.0
    counts = jnp.sum(onehot, axis=1, keepdims=True)
    rank = jnp.sum(onehot * earlier + lower * counts, axis=0, keepdims=True)
    return rank


def permute(table, rank):
    n = table.shape[1]
    place = lax.broadcasted_iota(jnp.int32, (n, n), 0).astype(F32)
    q = (rank == place).astype(F32)
    return lax.dot_general(
        table, q, (((1,), (1,)), ((), ())), precision=lax.Precision.HIGHEST, preferred_element_type=F32
    )


def place_of(rows, level):
    count = jnp.sum((rows[9:10] == float(level)).astype(F32)).astype(jnp.int32)
    start = jnp.sum((rows[9:10] < float(level)).astype(F32)).astype(jnp.int32)
    return start, count


def by_count(level, start, count, whole, packed):
    most = (96, 64, 0, 0)[level]
    if most == 0:
        pl.when(count > 0)(whole)
        return
    pl.when(count > most)(whole)

    @pl.when((count > 0) & (count <= most))
    def _():
        def step(k, c):
            packed(start + k * FEW, jnp.minimum(count - k * FEW, FEW))
            return c

        lax.fori_loop(0, (count + FEW - 1) >> SHIFT, step, 0)


def forward_kernel(base_ref, boxes_ref, targets_ref, image_ref, level_ref, label_ref, p2, p3, p4, p5, out_ref, sorted_ref, acc, acr, dwn, kone, ktwo, *, channels):
    pyr = (p2, p3, p4, p5)
    tile = pl.program_id(0)

    @pl.when(tile == 0)
    def _():
        count = boxes_ref.shape[1]
        table = jnp.concatenate(
            [
                targets_ref[...],
                boxes_ref[...],
                (image_ref[...] - base_ref[0]).astype(F32),
                level_ref[...].astype(F32),
                label_ref[...].astype(F32),
                jnp.zeros((5, count), F32),
            ]
        )
        rank = sort_tables(table)
        full = permute(table, rank)
        sorted_ref[0:16, :] = full
        sorted_ref[16:24, :] = jnp.broadcast_to(rank, (8, count))

    rows = sorted_ref[0:16, pl.ds(pl.multiple_of(tile * LANES, LANES), LANES)]
    acc[...] = jnp.zeros_like(acc)
    first = rows[8:9] == 0.0
    cells = POOL * POOL
    lane = lax.broadcasted_iota(jnp.int32, (1, LANES), 1)
    for level in range(4):
        extent = SIDE // 2**level
        size = extent * extent
        start, count = place_of(rows, level)

        def whole():
            write_tables(acr, dwn, rows, extent, level)

            def make(k_ref, i):
                kernel_row(k_ref, acr, dwn, i, extent, POOL)

            def use(k_ref, i):
                got = jnp.dot(pyr[level][...], k_ref[0:size, :], preferred_element_type=F32)
                sel = jnp.where(
                    jnp.concatenate([first] * POOL, 1), got[:channels], got[channels:]
                )
                for j in range(POOL):
                    at = pl.ds(i * POOL + j, channels, stride=cells)
                    acc[at, :] = acc[at, :] + sel[:, j * LANES : (j + 1) * LANES]

            over_rows((kone, ktwo), make, use)

        def packed(begin, number):
            few = pack_lanes(rows, begin)
            write_packed_tables(acr, dwn, few, extent, number)
            first_few = few[8:9] == 0.0
            inside = (lane >= begin) & (lane < begin + number)

            def make(k_ref, i):
                kernel_row(k_ref, acr, dwn, i, extent, PACKED)

            def use(k_ref, i):
                got = jnp.dot(
                    pyr[level][...], k_ref[0:size, 0 : PACKED * LANES], preferred_element_type=F32
                )
                sel = jnp.where(
                    jnp.concatenate([first_few] * PACKED, 1), got[:channels], got[channels:]
                )
                per = LANES // FEW
                for j in range(POOL):
                    at = pl.ds(i * POOL + j, channels, stride=cells)
                    piece = sel[:, (j // per) * LANES : (j // per + 1) * LANES]
                    piece = pltpu.roll(piece, lax.rem(begin + LANES - (j % per) * FEW, LANES), 1)
                    acc[at, :] = acc[at, :] + jnp.where(inside, piece, 0.0)

            over_rows((kone, ktwo), make, use)

        by_count(level, start, count, whole, packed)

    out_ref[...] = acc[...].astype(BF)


def pool_forward(base, boxes, targets, image, level, label, maps, channels):
    n = boxes.shape[1]
    rows = (boxes, targets, image, level, label)
    flat = channels * POOL * POOL
    full = lambda a: pl.BlockSpec(a.shape, lambda t: (0,) * a.ndim)
    return pl.pallas_call(
        functools.partial(forward_kernel, channels=channels),
        grid=(n // LANES,),
        in_specs=[pl.BlockSpec(memory_space=pltpu.SMEM)] + [full(a) for a in rows] + [full(m) for m in maps],
        out_specs=[
            pl.BlockSpec((flat, LANES), lambda t: (0, t)),
            pl.BlockSpec((24, n), lambda t: (0, 0)),
        ],
        out_shape=[
            jax.ShapeDtypeStruct((flat, n), BF),
            jax.ShapeDtypeStruct((24, n), F32),
        ],
        scratch_shapes=[
            pltpu.VMEM((flat, LANES), F32),
            pltpu.VMEM((POOL, SIDE, LANES), BF),
            pltpu.VMEM((POOL, SIDE, 16, LANES), BF),
            pltpu.VMEM((SIDE * SIDE, POOL * LANES), BF),
            pltpu.VMEM((SIDE * SIDE, POOL * LANES), BF),
        ],
        compiler_params=pltpu.CompilerParams(vmem_limit_bytes=VM),
        cost_estimate=pl.CostEstimate(flops=40 * 10**9, bytes_accessed=10**7, transcendentals=0),
        name="pool_forward",
    )(base, *rows, *maps)


def backward_kernel(sorted_ref, gp_ref, o2, o3, o4, o5, g32, acr, dwn, kone, ktwo, gbuf, *, channels):
    outs = (o2, o3, o4, o5)
    tile = pl.program_id(0)

    @pl.when(tile == 0)
    def _():
        for o in outs:
            o[...] = jnp.zeros_like(o)

    rows = sorted_ref[0:16, pl.ds(pl.multiple_of(tile * LANES, LANES), LANES)]
    g32[...] = gp_ref[...].astype(F32) * (1.0 / 3.0)
    first = rows[8:9] == 0.0
    cells = POOL * POOL
    lane = lax.broadcasted_iota(jnp.int32, (1, LANES), 1)
    for level in range(4):
        extent = SIDE // 2**level
        size = extent * extent
        start, count = place_of(rows, level)

        def whole():
            write_tables(acr, dwn, rows, extent, level)

            def make(k_ref, i):
                kernel_row(k_ref, acr, dwn, i, extent, POOL)

            def use(k_ref, i):
                for j in range(POOL):
                    g = g32[pl.ds(i * POOL + j, channels, stride=cells), :]
                    gbuf[0:channels, j * LANES : (j + 1) * LANES] = jnp.where(first, g, 0.0).astype(BF)
                    gbuf[channels:, j * LANES : (j + 1) * LANES] = jnp.where(first, 0.0, g).astype(BF)
                outs[level][...] += lax.dot_general(
                    gbuf[...], k_ref[0:size, :], (((1,), (1,)), ((), ())), preferred_element_type=F32
                )

            over_rows((kone, ktwo), make, use)

        def packed(begin, number):
            few = pack_lanes(rows, begin)
            write_packed_tables(acr, dwn, few, extent, number)
            first_few = few[8:9] == 0.0

            def make(k_ref, i):
                kernel_row(k_ref, acr, dwn, i, extent, PACKED)

            def use(k_ref, i):
                per = LANES // FEW
                for t in range(PACKED):
                    g = jnp.zeros((channels, LANES), F32)
                    for j in range(t * per, min(POOL, (t + 1) * per)):
                        piece = g32[pl.ds(i * POOL + j, channels, stride=cells), :]
                        shift = lax.rem((j % per) * FEW + LANES - begin, LANES)
                        here = (lane >> SHIFT) == j % per
                        g = jnp.where(here, pltpu.roll(piece, shift, 1), g)
                    at = slice(t * LANES, (t + 1) * LANES)
                    gbuf[0:channels, at] = jnp.where(first_few, g, 0.0).astype(BF)
                    gbuf[channels:, at] = jnp.where(first_few, 0.0, g).astype(BF)
                outs[level][...] += lax.dot_general(
                    gbuf[:, 0 : PACKED * LANES],
                    k_ref[0:size, 0 : PACKED * LANES],
                    (((1,), (1,)), ((), ())),
                    preferred_element_type=F32,
                )

            over_rows((kone, ktwo), make, use)

        by_count(level, start, count, whole, packed)


def pool_backward(sorted_table, gp, channels):
    n = sorted_table.shape[1]
    flat = channels * POOL * POOL
    sizes = [(SIDE // 2**l) ** 2 for l in range(4)]
    return pl.pallas_call(
        functools.partial(backward_kernel, channels=channels),
        grid=(n // LANES,),
        in_specs=[
            pl.BlockSpec(sorted_table.shape, lambda t: (0, 0)),
            pl.BlockSpec((flat, LANES), lambda t: (0, t)),
        ],
        out_specs=[pl.BlockSpec((2 * channels, s), lambda t: (0, 0)) for s in sizes],
        out_shape=[jax.ShapeDtypeStruct((2 * channels, s), F32) for s in sizes],
        scratch_shapes=[
            pltpu.VMEM((flat, LANES), F32),
            pltpu.VMEM((POOL, SIDE, LANES), BF),
            pltpu.VMEM((POOL, SIDE, 16, LANES), BF),
            pltpu.VMEM((SIDE * SIDE, POOL * LANES), BF),
            pltpu.VMEM((SIDE * SIDE, POOL * LANES), BF),
            pltpu.VMEM((2 * channels, POOL * LANES), BF),
        ],
        compiler_params=pltpu.CompilerParams(vmem_limit_bytes=VM),
        cost_estimate=pl.CostEstimate(flops=40 * 10**9, bytes_accessed=10**7, transcendentals=0),
        name="pool_backward",
    )(sorted_table, gp)


BOX = 96
ROOT = 0.7071067811865476
DENSITY = 0.3989422804014327
STRIP = 16


def unit_and_slope(x):
    below = 0.5 + 0.5 * lax.erf(x * ROOT)
    return x * below, below + x * jnp.exp(-0.5 * x * x) * DENSITY


def strips(rows, work, carry):
    def step(k, c):
        return work(pl.ds(pl.multiple_of(k * STRIP, STRIP), STRIP), c)

    return lax.fori_loop(0, rows // STRIP, step, carry)


def head_kernel(
    part_ref,
    ordered_ref,
    own_ref,
    other_ref,
    bias_one,
    weight_two,
    bias_two,
    weight_out,
    bias_out,
    grad_one,
    grad_two_weight,
    small,
    last,
    decoded_ref,
    act_one,
    act_two,
    grad_two,
    slope_one,
    slope_two,
    wide,
    *,
    classes,
    norm,
):
    rows, hidden = own_ref.shape
    lanes = weight_out.shape[1]

    def one(at, c):
        x = own_ref[at, :].astype(F32) + other_ref[at, :].astype(F32) + bias_one[...]
        act, slope = unit_and_slope(x)
        act_one[at, :] = act.astype(BF)
        slope_one[at, :] = slope
        return c

    strips(rows, one, 0)
    wide[...] = jnp.dot(act_one[...], weight_two[...], preferred_element_type=F32)

    def two(at, c):
        act, slope = unit_and_slope(wide[at, :] + bias_two[...])
        act_two[at, :] = act.astype(BF)
        slope_two[at, :] = slope
        return c

    strips(rows, two, 0)
    out = jnp.dot(act_two[...], weight_out[...], preferred_element_type=F32) + bias_out[...]
    ordered = ordered_ref[...]
    aux = jnp.concatenate(
        [
            jnp.zeros((BOX - 8, rows), F32),
            ordered[8:16],
            ordered[0:8],
            jnp.zeros((lanes - BOX - 8, rows), F32),
        ]
    ).T
    lane = lax.broadcasted_iota(jnp.int32, (rows, lanes), 1)
    is_class = lane < classes
    is_box = (lane >= BOX) & (lane < BOX + 4)
    label = aux[:, BOX - 6 : BOX - 5]
    hit = (lane.astype(F32) == label).astype(F32)
    fore = (label < classes - 1.0).astype(F32)
    scores = jnp.where(is_class, out, -3.0e38)
    top = jnp.max(scores, axis=1, keepdims=True)
    powers = jnp.where(is_class, jnp.exp(scores - top), 0.0)
    total = jnp.sum(powers, axis=1, keepdims=True)
    chosen = jnp.sum(jnp.where(is_class, out * hit, 0.0), axis=1, keepdims=True)
    class_loss = jnp.sum(top + jnp.log(total) - chosen, axis=0, keepdims=True) / norm
    residue = out - aux
    size = jnp.abs(residue)
    huber = jnp.where(size < 1.0, 0.5 * residue * residue, size - 0.5)
    huber = jnp.sum(jnp.where(is_box, huber, 0.0), axis=1, keepdims=True) * fore
    box_loss = jnp.sum(huber, axis=0, keepdims=True) / norm
    grad_out = jnp.where(
        is_class,
        (powers / total - hit) / norm,
        jnp.where(is_box, fore * jnp.clip(residue, -1.0, 1.0) / norm, 0.0),
    ).astype(BF)
    bias_sums = jnp.sum(grad_out.astype(F32), axis=0, keepdims=True)
    last[...] = jnp.concatenate(
        [
            bias_sums,
            jnp.broadcast_to(class_loss, (1, lanes)),
            jnp.broadcast_to(box_loss, (1, lanes)),
            jnp.zeros((5, lanes), F32),
        ]
    )
    moves = out.T[BOX : BOX + 4]
    x1, y1, x2, y2 = (ordered[k : k + 1] for k in range(4, 8))
    width, height = x2 - x1, y2 - y1
    px = moves[0:1] / 10.0 * width + (x1 + 0.5 * width)
    py = moves[1:2] / 10.0 * height + (y1 + 0.5 * height)
    half_w = 0.5 * (jnp.exp(moves[2:3] / 5.0) * width)
    half_h = 0.5 * (jnp.exp(moves[3:4] / 5.0) * height)
    boxes = jnp.concatenate(
        [px - half_w, py - half_h, px + half_w, py + half_h, jnp.zeros((4, rows), F32)]
    )
    place = lax.broadcasted_iota(jnp.int32, (rows, rows), 0).astype(F32)
    back = (ordered_ref[16:17, :] == place).astype(F32)
    decoded_ref[...] = jnp.dot(
        boxes, back, precision=lax.Precision.HIGHEST, preferred_element_type=F32
    )
    wide[...] = lax.dot_general(
        grad_out, weight_out[...], (((1,), (1,)), ((), ())), preferred_element_type=F32
    )

    def three(at, c):
        g = (wide[at, :] * slope_two[at, :]).astype(BF)
        grad_two[at, :] = g
        g = g.astype(F32)
        return c + g[0:8] + g[8:16]

    bias_two_sum = strips(rows, three, jnp.zeros((8, hidden), F32))
    wide[...] = lax.dot_general(
        grad_two[...], weight_two[...], (((1,), (1,)), ((), ())), preferred_element_type=F32
    )

    def four(at, c):
        g = (wide[at, :] * slope_one[at, :]).astype(BF)
        grad_one[at, :] = g
        g = g.astype(F32)
        return c + g[0:8] + g[8:16]

    bias_one_sum = strips(rows, four, jnp.zeros((8, hidden), F32))
    part = grad_two_weight.shape[0]
    columns = pl.ds(pl.multiple_of(part_ref[0] * part, part), part)
    grad_two_weight[...] = lax.dot_general(
        act_one[:, columns], grad_two[...], (((0,), (0,)), ((), ())), preferred_element_type=F32
    ).astype(BF)
    products = lax.dot_general(
        grad_out, act_two[...], (((0,), (0,)), ((), ())), preferred_element_type=F32
    )
    sums = jnp.concatenate(
        [
            jnp.sum(bias_one_sum, axis=0, keepdims=True),
            jnp.sum(bias_two_sum, axis=0, keepdims=True),
            jnp.zeros((lanes - BOX - 10, hidden), F32),
        ]
    )
    small[...] = jnp.concatenate([products[: BOX + 8], sums]).astype(BF)


def head_pass(
    part, parts, ordered, own, other, bias_one, weight_two, bias_two, weight_out, bias_out, classes, norm
):
    rows, hidden = own.shape
    lanes = weight_out.shape[1]
    whole = pl.BlockSpec(memory_space=pltpu.VMEM)
    return pl.pallas_call(
        functools.partial(head_kernel, classes=classes, norm=norm),
        in_specs=[pl.BlockSpec(memory_space=pltpu.SMEM)] + [whole] * 8,
        out_specs=[whole] * 5,
        out_shape=[
            jax.ShapeDtypeStruct((rows, hidden), BF),
            jax.ShapeDtypeStruct((hidden // parts, hidden), BF),
            jax.ShapeDtypeStruct((lanes, hidden), BF),
            jax.ShapeDtypeStruct((8, lanes), F32),
            jax.ShapeDtypeStruct((8, rows), F32),
        ],
        scratch_shapes=[pltpu.VMEM((rows, hidden), BF)] * 3 + [pltpu.VMEM((rows, hidden), F32)] * 3,
        compiler_params=pltpu.CompilerParams(vmem_limit_bytes=VM),
        cost_estimate=pl.CostEstimate(
            flops=6 * rows * hidden * hidden, bytes_accessed=8 * rows * hidden, transcendentals=0
        ),
        name="head",
    )(part, ordered, own, other, bias_one, weight_two, bias_two, weight_out, bias_out)


def partners(stride):
    return [(k, k ^ stride) for k in range(lax.axis_size("roi"))]


def halve(sums, axis, stride, size, with_last=False):
    while size > 1:
        mine = (lax.axis_index("roi") // stride) % 2
        shape = sums.shape
        split = sums.reshape(shape[:axis] + (size // 2, 2) + shape[axis + 1 :])
        keep = lax.dynamic_index_in_dim(split, mine, axis + 1, False)
        send = lax.dynamic_index_in_dim(split, 1 - mine, axis + 1, False)
        come = lax.ppermute(send, "roi", partners(stride))
        sums = (keep.astype(F32) + come.astype(F32)).astype(BF)
        stride, size = 2 * stride, size // 2
    sums = lax.squeeze(sums, (axis,))
    return (sums, come) if with_last else sums


def add_up_everywhere(values):
    stride = 1
    while stride < lax.axis_size("roi"):
        values = values + lax.ppermute(values, "roi", partners(stride))
        stride *= 2
    return values


def row_parts(rows):
    unit = 8 if rows % 8 == 0 else 1
    units = rows // unit
    cuts = [0, units * 47 // 100, units * 4 // 5, units]
    return [unit * (b - a) for a, b in zip(cuts, cuts[1:])]


def spread_out(mine):
    stride, axis, shape = lax.axis_size("roi") // 2, 0, mine.shape
    while stride:
        low = (lax.axis_index("roi") // stride) % 2 == 0
        come = lax.ppermute(mine, "roi", partners(stride))
        mine = jnp.stack([jnp.where(low, mine, come), jnp.where(low, come, mine)], axis)
        stride, axis = stride // 2, axis + 1
    return mine.reshape(-1, shape[-1])


def after(value, *earlier):
    anywhere = pl.BlockSpec(memory_space=pl.ANY)
    return pl.pallas_call(
        lambda *refs: None,
        in_specs=[anywhere] * (1 + len(earlier)),
        out_specs=anywhere,
        out_shape=jax.ShapeDtypeStruct(value.shape, value.dtype),
        input_output_aliases={0: 0},
        cost_estimate=pl.CostEstimate(flops=0, bytes_accessed=0, transcendentals=0),
        name="after",
    )(value, *earlier)


def swap_rows_kernel(core_ref, pooled_ref, done_ref, send_ref):
    send_ref[...] = pooled_ref[0]


def rows_to_send(core, by_core, done):
    blocks, _, share, regions = by_core.shape
    return pl.pallas_call(
        swap_rows_kernel,
        grid_spec=pltpu.PrefetchScalarGridSpec(
            num_scalar_prefetch=1,
            grid=(blocks,),
            in_specs=[
                pl.BlockSpec((1, 1, share, regions), lambda k, c: (k, 1 - c[0], 0, 0)),
                pl.BlockSpec(memory_space=pl.ANY),
            ],
            out_specs=pl.BlockSpec((1, share, regions), lambda k, c: (k, 0, 0)),
        ),
        out_shape=jax.ShapeDtypeStruct((blocks, share, regions), by_core.dtype),
        compiler_params=pltpu.CompilerParams(vmem_limit_bytes=VM),
        cost_estimate=pl.CostEstimate(
            flops=0, bytes_accessed=4 * blocks * share * regions, transcendentals=0
        ),
        name="rows_to_send",
    )(core, by_core, done)


def join_kernel(core_ref, mine_ref, theirs_ref, *outs, split):
    regions = theirs_ref.shape[-1]
    at = 0
    for rows, out in zip(split, outs):
        out[0, :, :regions] = mine_ref[0, 0, at : at + rows]
        out[0, :, regions:] = theirs_ref[0, at : at + rows]
        at += rows


def join_regions(core, by_core, theirs, split):
    blocks, _, share, regions = by_core.shape
    return pl.pallas_call(
        functools.partial(join_kernel, split=split),
        grid_spec=pltpu.PrefetchScalarGridSpec(
            num_scalar_prefetch=1,
            grid=(blocks,),
            in_specs=[
                pl.BlockSpec((1, 1, share, regions), lambda k, c: (k, c[0], 0, 0)),
                pl.BlockSpec((1, share, regions), lambda k, c: (k, 0, 0)),
            ],
            out_specs=[
                pl.BlockSpec((1, rows, 2 * regions), lambda k, c: (k, 0, 0)) for rows in split
            ],
        ),
        out_shape=[
            jax.ShapeDtypeStruct((blocks, rows, 2 * regions), by_core.dtype) for rows in split
        ],
        compiler_params=pltpu.CompilerParams(vmem_limit_bytes=VM),
        cost_estimate=pl.CostEstimate(
            flops=0, bytes_accessed=8 * blocks * share * regions, transcendentals=0
        ),
        name="join_regions",
    )(core, by_core, theirs)


def on_device(
    pyramid_two,
    pyramid_three,
    pyramid_four,
    pyramid_five,
    proposals,
    image_index,
    levels,
    labels,
    targets,
    first_weight,
    first_bias,
    second_weight,
    second_bias,
    class_weight,
    class_bias,
    box_weight,
    box_bias,
):
    features = (pyramid_two, pyramid_three, pyramid_four, pyramid_five)
    images_here, channels_here = (pyramid_two.shape[0], pyramid_two.shape[1])
    regions_here = proposals.shape[1]
    ways, groups = lax.axis_size("roi"), lax.axis_size("ch")
    outer, inner = 4, ways // 8
    flat, hidden = first_weight.shape
    classes = class_weight.shape[1]
    share = flat // ways
    core = lax.axis_index("roi") % 2
    group = lax.axis_index("ch")
    maps = [f.reshape(images_here * channels_here, -1) for f in features]
    base = jnp.reshape(lax.axis_index("roi") * images_here, (1,)).astype(jnp.int32)
    pooled, ordered = pool_forward(
        base, proposals, targets, image_index[None], levels[None], labels[None], maps, channels_here
    )
    partial = lax.dot_general(
        pooled, first_weight, (((0,), (0,)), ((), ())), preferred_element_type=F32
    )
    if groups == 2:
        partial = partial.astype(BF)
        other = lax.ppermute(partial, "ch", [(0, 1), (1, 0)])
    else:
        partial = lax.psum(partial, "ch")
        other = jnp.zeros(partial.shape, BF)
    core = jnp.reshape(core, (1,)).astype(jnp.int32)
    by_core = pooled.reshape(ways // 2, 2, share, regions_here)
    theirs = lax.ppermute(rows_to_send(core, by_core, partial), "roi", partners(1))
    split = row_parts(share)
    both = join_regions(core, by_core, theirs, split)
    gap = jnp.zeros((hidden, BOX - classes), BF)
    tail = jnp.zeros((hidden, 128 - BOX - 4), BF)
    weight_out = jnp.concatenate([class_weight, gap, box_weight, tail], 1)
    bias_out = jnp.concatenate([class_bias, gap[0], box_bias, tail[0]]).astype(F32)[None]
    grad_pre_one, grad_two, small, last, decoded = head_pass(
        jnp.reshape(group, (1,)).astype(jnp.int32),
        groups,
        after(ordered, both[0]),
        partial,
        other,
        first_bias.astype(F32)[None],
        second_weight,
        second_bias.astype(F32)[None],
        weight_out,
        bias_out,
        classes,
        float(regions_here * ways),
    )
    grad_both = jnp.concatenate([grad_pre_one, lax.ppermute(grad_pre_one, "roi", partners(1))], 0)
    first, second, third = (
        jnp.dot(b.reshape(-1, 2 * regions_here), grad_both, preferred_element_type=F32)
        .astype(BF)
        .reshape(outer, inner, -1, hidden)
        for b in both
    )
    extra = jnp.concatenate([grad_two, small])
    extra_share = extra.shape[0] // ways
    extra = halve(extra.reshape(ways // 2, 2, extra_share, hidden), 1, 1, 2)
    extra = extra.reshape(outer, inner, extra_share, hidden)
    third = jnp.concatenate([third, extra], 2)
    first, arrived = halve(first, 1, 2, inner, True)
    second, _ = halve(after(second, arrived), 1, 2, inner, True)
    first_sum = halve(first, 0, 2 * inner, outer)
    second_sum = halve(second, 0, 2 * inner, outer)
    third_sum = halve(halve(third, 0, 2 * inner, outer), 0, 2, inner)
    share_sum = jnp.concatenate([first_sum, second_sum, third_sum[: split[2]]])
    grad_weight_one = lax.all_gather(share_sum, "roi", tiled=True).astype(F32)
    extra = spread_out(third_sum[split[2] :])
    part_rows = hidden // groups
    small = extra[part_rows:].astype(F32)
    if groups == 2:
        two = extra[:part_rows]
        two_other = lax.ppermute(two, "ch", [(0, 1), (1, 0)])
        two = jnp.concatenate(
            [jnp.where(group == 0, two, two_other), jnp.where(group == 0, two_other, two)]
        )
    else:
        two = lax.all_gather(extra[:part_rows], "ch", tiled=True)
    grad_pooled = lax.dot_general(
        first_weight, grad_pre_one, (((1,), (1,)), ((), ())), preferred_element_type=F32
    ).astype(BF)
    last = add_up_everywhere(last)
    share_rows = regions_here // groups
    decoded = lax.dynamic_slice(decoded, (0, group * share_rows), (4, share_rows))
    map_grads = pool_backward(ordered, grad_pooled, channels_here)
    pyramid_grads = [g.reshape(f.shape) for g, f in zip(map_grads, features)]
    return (
        last[1, 0],
        last[2, 0],
        decoded,
        grad_weight_one,
        small[BOX + 8],
        two.astype(F32),
        small[BOX + 9],
        small[:classes].T,
        last[0, :classes],
        small[BOX : BOX + 4].T,
        last[0, BOX : BOX + 4],
        pyramid_grads[0],
        pyramid_grads[1],
        pyramid_grads[2],
        pyramid_grads[3],
    )


def solution(mesh):
    return jax.shard_map(
        on_device,
        mesh=mesh,
        in_specs=(
            P("roi", "ch", None),
            P("roi", "ch", None),
            P("roi", "ch", None),
            P("roi", "ch", None),
            P(None, "roi"),
            P("roi"),
            P("roi"),
            P("roi"),
            P(None, "roi"),
            P("ch", None),
            P(),
            P(),
            P(),
            P(),
            P(),
            P(),
            P(),
        ),
        out_specs=(
            P(),
            P(),
            P(None, ("roi", "ch")),
            P("ch", None),
            P(),
            P(),
            P(),
            P(),
            P(),
            P(),
            P(),
            P("roi", "ch", None),
            P("roi", "ch", None),
            P("roi", "ch", None),
            P("roi", "ch", None),
        ),
        check_vma=False,
    )
```

```python
import functools
import jax, jax.numpy as jnp
from jax import lax
from jax.sharding import PartitionSpec as P
from jax.experimental import pallas as pl
from jax.experimental.pallas import tpu as pltpu

POOL = 7
SAMPLES = 2
SIDE = 64
LANES = 128
SUBLANES = 8
FEW = 32
PACKED = 2
SHIFT = 5
BF = jnp.bfloat16
F32 = jnp.float32
VM = 60 * 2**20
VM_POOL = 60 * 2**20


def spread_one(low, high, extent, col):
    anchor = low * extent - 0.5
    stride = (high - low) * extent / POOL
    places = lax.broadcasted_iota(jnp.int32, (extent, LANES), 0).astype(F32)
    total = None
    for s in range(SAMPLES):
        at = jnp.clip(anchor + (col + (s + 0.5) / SAMPLES) * stride, 0.0, extent - 1.0)
        term = jnp.maximum(0.0, 1.0 - jnp.abs(at - places))
        total = term if total is None else total + term
    return total / SAMPLES


def spread(low, high, extent):
    return [spread_one(low, high, extent, float(col)) for col in range(POOL)]


def write_down(down_ref, rows, extent):
    down = spread(rows[5:6], rows[7:8], extent)
    for i in range(POOL):
        d = down[i]
        if extent < 16:
            half = lax.broadcasted_iota(jnp.int32, (16, LANES), 0) < extent
            for q in range(extent // 2):
                top = jnp.broadcast_to(d[2 * q : 2 * q + 1], (16, LANES))
                low = jnp.broadcast_to(d[2 * q + 1 : 2 * q + 2], (16, LANES))
                down_ref[i, q] = jnp.where(half, top, low).astype(BF)
        else:
            for h in range(extent):
                down_ref[i, h] = jnp.broadcast_to(d[h : h + 1], (16, LANES)).astype(BF)


def write_across(across_ref, index, weights, mask, extent):
    a = (weights * mask).astype(BF).astype(F32)
    if extent < 16:
        a = jnp.concatenate([a] * (16 // extent), 0)
    across_ref[index, 0 : max(extent, 16), :] = a.astype(BF)


def write_tables(across_ref, down_ref, rows, extent, level):
    mask = (rows[9:10] == float(level)).astype(F32)
    across = spread(rows[4:5], rows[6:7], extent)
    for j in range(POOL):
        write_across(across_ref, j, across[j], mask, extent)
    write_down(down_ref, rows, extent)


def pack_lanes(rows, start):
    lane = lax.broadcasted_iota(jnp.int32, rows.shape, 1)
    rolled = pltpu.roll(rows, lax.rem(LANES - start, LANES), 1)
    few = jnp.where(lane < FEW, rolled, 0.0)
    total = few
    for k in range(1, LANES // FEW):
        total = total + pltpu.roll(few, k * FEW, 1)
    return total


def write_packed_tables(across_ref, down_ref, rows, extent, count):
    lane = lax.broadcasted_iota(jnp.int32, (1, LANES), 1)
    mask = ((lane & (FEW - 1)) < count).astype(F32)
    per = LANES // FEW
    for t in range(PACKED):
        column = (lane >> SHIFT) + t * per
        across = spread_one(rows[4:5], rows[6:7], extent, column.astype(F32))
        write_across(across_ref, t, across, mask * (column < POOL).astype(F32), extent)
    write_down(down_ref, rows, extent)


def kernel_row(k_ref, across_ref, down_ref, i, extent, lane_tiles):
    wide = max(extent, 16)
    tiles = extent * extent // wide
    down = down_ref[i, 0:tiles].reshape(tiles, 1, 16, LANES)
    for j in range(lane_tiles):
        across = across_ref[j, 0:wide, :].reshape(1, wide // 16, 16, LANES)
        k_ref[0 : extent * extent, j * LANES : (j + 1) * LANES] = (across * down).reshape(
            extent * extent, LANES
        )


def over_rows(k_refs, make, use):
    first, second = k_refs
    make(first, 0)

    def pair(p, c):
        make(second, 2 * p + 1)
        use(first, 2 * p)
        make(first, 2 * p + 2)
        use(second, 2 * p + 1)
        return c

    lax.fori_loop(0, POOL // 2, pair, 0)
    use(first, POOL - 1)


def sort_tables(table):
    n = table.shape[1]
    level = table[9:10]
    which = lax.broadcasted_iota(jnp.int32, (8, n), 0).astype(F32)
    onehot = (level == which).astype(F32)
    before = (
        lax.broadcasted_iota(jnp.int32, (n, n), 0) < lax.broadcasted_iota(jnp.int32, (n, n), 1)
    ).astype(BF)
    earlier = jnp.dot(onehot.astype(BF), before, preferred_element_type=F32)
    lower = (which < level).astype(F32) * 1.0
    counts = jnp.sum(onehot, axis=1, keepdims=True)
    rank = jnp.sum(onehot * earlier + lower * counts, axis=0, keepdims=True)
    return rank


def permute(table, rank):
    n = table.shape[1]
    place = lax.broadcasted_iota(jnp.int32, (n, n), 0).astype(F32)
    q = (rank == place).astype(F32)
    return lax.dot_general(
        table, q, (((1,), (1,)), ((), ())), precision=lax.Precision.HIGHEST, preferred_element_type=F32
    )


def place_of(rows, level):
    count = jnp.sum((rows[9:10] == float(level)).astype(F32)).astype(jnp.int32)
    start = jnp.sum((rows[9:10] < float(level)).astype(F32)).astype(jnp.int32)
    return start, count


def by_count(level, start, count, whole, packed):
    most = (96, 64, 0, 0)[level]
    if most == 0:
        pl.when(count > 0)(whole)
        return
    pl.when(count > most)(whole)

    @pl.when((count > 0) & (count <= most))
    def _():
        def step(k, c):
            packed(start + k * FEW, jnp.minimum(count - k * FEW, FEW))
            return c

        lax.fori_loop(0, (count + FEW - 1) >> SHIFT, step, 0)


def forward_kernel(base_ref, boxes_ref, targets_ref, image_ref, level_ref, label_ref, p2, p3, p4, p5, out_ref, send_ref, sorted_ref, acc, acr, dwn, kone, ktwo, *, channels):
    pyr = (p2, p3, p4, p5)
    tile = pl.program_id(0)

    @pl.when(tile == 0)
    def _():
        count = boxes_ref.shape[1]
        table = jnp.concatenate(
            [
                targets_ref[...],
                boxes_ref[...],
                (image_ref[...] - base_ref[0]).astype(F32),
                level_ref[...].astype(F32),
                label_ref[...].astype(F32),
                jnp.zeros((5, count), F32),
            ]
        )
        rank = sort_tables(table)
        full = permute(table, rank)
        sorted_ref[0:16, :] = full
        sorted_ref[16:24, :] = jnp.broadcast_to(rank, (8, count))

    rows = sorted_ref[0:16, pl.ds(pl.multiple_of(tile * LANES, LANES), LANES)]
    acc[...] = jnp.zeros_like(acc)
    first = rows[8:9] == 0.0
    cells = POOL * POOL
    lane = lax.broadcasted_iota(jnp.int32, (1, LANES), 1)
    for level in range(4):
        extent = SIDE // 2**level
        size = extent * extent
        start, count = place_of(rows, level)

        def whole():
            write_tables(acr, dwn, rows, extent, level)

            def make(k_ref, i):
                kernel_row(k_ref, acr, dwn, i, extent, POOL)

            def use(k_ref, i):
                got = jnp.dot(pyr[level][...], k_ref[0:size, :], preferred_element_type=F32)
                sel = jnp.where(
                    jnp.concatenate([first] * POOL, 1), got[:channels], got[channels:]
                )
                for j in range(POOL):
                    at = pl.ds(i * POOL + j, channels, stride=cells)
                    acc[at, :] = acc[at, :] + sel[:, j * LANES : (j + 1) * LANES]

            over_rows((kone, ktwo), make, use)

        def packed(begin, number):
            few = pack_lanes(rows, begin)
            write_packed_tables(acr, dwn, few, extent, number)
            first_few = few[8:9] == 0.0
            inside = (lane >= begin) & (lane < begin + number)

            def make(k_ref, i):
                kernel_row(k_ref, acr, dwn, i, extent, PACKED)

            def use(k_ref, i):
                got = jnp.dot(
                    pyr[level][...], k_ref[0:size, 0 : PACKED * LANES], preferred_element_type=F32
                )
                sel = jnp.where(
                    jnp.concatenate([first_few] * PACKED, 1), got[:channels], got[channels:]
                )
                per = LANES // FEW
                for j in range(POOL):
                    at = pl.ds(i * POOL + j, channels, stride=cells)
                    piece = sel[:, (j // per) * LANES : (j // per + 1) * LANES]
                    piece = pltpu.roll(piece, lax.rem(begin + LANES - (j % per) * FEW, LANES), 1)
                    acc[at, :] = acc[at, :] + jnp.where(inside, piece, 0.0)

            over_rows((kone, ktwo), make, use)

        by_count(level, start, count, whole, packed)

    out_ref[...] = acc[...].astype(BF)
    blocks, share = send_ref.shape[0:2]
    for k in range(blocks):
        at = pl.multiple_of((2 * k + 1 - base_ref[1]) * share, SUBLANES if share % SUBLANES == 0 else 1)
        send_ref[k] = acc[pl.ds(at, share), :].astype(BF)


def pool_forward(base, boxes, targets, image, level, label, maps, channels):
    n = boxes.shape[1]
    ways = lax.axis_size("roi")
    rows = (boxes, targets, image, level, label)
    flat = channels * POOL * POOL
    full = lambda a: pl.BlockSpec(a.shape, lambda t: (0,) * a.ndim)
    return pl.pallas_call(
        functools.partial(forward_kernel, channels=channels),
        grid=(n // LANES,),
        in_specs=[pl.BlockSpec(memory_space=pltpu.SMEM)] + [full(a) for a in rows] + [full(m) for m in maps],
        out_specs=[
            pl.BlockSpec((flat, LANES), lambda t: (0, t)),
            pl.BlockSpec((ways // 2, flat // ways, LANES), lambda t: (0, 0, t)),
            pl.BlockSpec((24, n), lambda t: (0, 0)),
        ],
        out_shape=[
            jax.ShapeDtypeStruct((flat, n), BF),
            jax.ShapeDtypeStruct((ways // 2, flat // ways, n), BF),
            jax.ShapeDtypeStruct((24, n), F32),
        ],
        scratch_shapes=[
            pltpu.VMEM((flat, LANES), F32),
            pltpu.VMEM((POOL, SIDE, LANES), BF),
            pltpu.VMEM((POOL, SIDE, 16, LANES), BF),
            pltpu.VMEM((SIDE * SIDE, POOL * LANES), BF),
            pltpu.VMEM((SIDE * SIDE, POOL * LANES), BF),
        ],
        compiler_params=pltpu.CompilerParams(vmem_limit_bytes=VM_POOL),
        cost_estimate=pl.CostEstimate(flops=40 * 10**9, bytes_accessed=10**7, transcendentals=0),
        name="pool_forward",
    )(base, *rows, *maps)


def backward_kernel(sorted_ref, gp_ref, o2, o3, o4, o5, g32, acr, dwn, kone, ktwo, gbuf, *, channels):
    outs = (o2, o3, o4, o5)
    tile = pl.program_id(0)

    @pl.when(tile == 0)
    def _():
        for o in outs:
            o[...] = jnp.zeros_like(o)

    rows = sorted_ref[0:16, pl.ds(pl.multiple_of(tile * LANES, LANES), LANES)]
    g32[...] = gp_ref[...].astype(F32) * (1.0 / 3.0)
    first = rows[8:9] == 0.0
    cells = POOL * POOL
    lane = lax.broadcasted_iota(jnp.int32, (1, LANES), 1)
    for level in range(4):
        extent = SIDE // 2**level
        size = extent * extent
        start, count = place_of(rows, level)

        def whole():
            write_tables(acr, dwn, rows, extent, level)

            def make(k_ref, i):
                kernel_row(k_ref, acr, dwn, i, extent, POOL)

            def use(k_ref, i):
                for j in range(POOL):
                    g = g32[pl.ds(i * POOL + j, channels, stride=cells), :]
                    gbuf[0:channels, j * LANES : (j + 1) * LANES] = jnp.where(first, g, 0.0).astype(BF)
                    gbuf[channels:, j * LANES : (j + 1) * LANES] = jnp.where(first, 0.0, g).astype(BF)
                outs[level][...] += lax.dot_general(
                    gbuf[...], k_ref[0:size, :], (((1,), (1,)), ((), ())), preferred_element_type=F32
                )

            over_rows((kone, ktwo), make, use)

        def packed(begin, number):
            few = pack_lanes(rows, begin)
            write_packed_tables(acr, dwn, few, extent, number)
            first_few = few[8:9] == 0.0

            def make(k_ref, i):
                kernel_row(k_ref, acr, dwn, i, extent, PACKED)

            def use(k_ref, i):
                per = LANES // FEW
                for t in range(PACKED):
                    g = jnp.zeros((channels, LANES), F32)
                    for j in range(t * per, min(POOL, (t + 1) * per)):
                        piece = g32[pl.ds(i * POOL + j, channels, stride=cells), :]
                        shift = lax.rem((j % per) * FEW + LANES - begin, LANES)
                        here = (lane >> SHIFT) == j % per
                        g = jnp.where(here, pltpu.roll(piece, shift, 1), g)
                    at = slice(t * LANES, (t + 1) * LANES)
                    gbuf[0:channels, at] = jnp.where(first_few, g, 0.0).astype(BF)
                    gbuf[channels:, at] = jnp.where(first_few, 0.0, g).astype(BF)
                outs[level][...] += lax.dot_general(
                    gbuf[:, 0 : PACKED * LANES],
                    k_ref[0:size, 0 : PACKED * LANES],
                    (((1,), (1,)), ((), ())),
                    preferred_element_type=F32,
                )

            over_rows((kone, ktwo), make, use)

        by_count(level, start, count, whole, packed)


def pool_backward(sorted_table, gp, channels):
    n = sorted_table.shape[1]
    flat = channels * POOL * POOL
    sizes = [(SIDE // 2**l) ** 2 for l in range(4)]
    return pl.pallas_call(
        functools.partial(backward_kernel, channels=channels),
        grid=(n // LANES,),
        in_specs=[
            pl.BlockSpec(sorted_table.shape, lambda t: (0, 0)),
            pl.BlockSpec((flat, LANES), lambda t: (0, t)),
        ],
        out_specs=[pl.BlockSpec((2 * channels, s), lambda t: (0, 0)) for s in sizes],
        out_shape=[jax.ShapeDtypeStruct((2 * channels, s), F32) for s in sizes],
        scratch_shapes=[
            pltpu.VMEM((flat, LANES), F32),
            pltpu.VMEM((POOL, SIDE, LANES), BF),
            pltpu.VMEM((POOL, SIDE, 16, LANES), BF),
            pltpu.VMEM((SIDE * SIDE, POOL * LANES), BF),
            pltpu.VMEM((SIDE * SIDE, POOL * LANES), BF),
            pltpu.VMEM((2 * channels, POOL * LANES), BF),
        ],
        compiler_params=pltpu.CompilerParams(vmem_limit_bytes=VM),
        cost_estimate=pl.CostEstimate(flops=40 * 10**9, bytes_accessed=10**7, transcendentals=0),
        name="pool_backward",
    )(sorted_table, gp)


BOX = 96
ROOT = 0.7071067811865476
DENSITY = 0.3989422804014327
STRIP = 16


def unit_and_slope(x):
    below = 0.5 + 0.5 * lax.erf(x * ROOT)
    return x * below, below + x * jnp.exp(-0.5 * x * x) * DENSITY


def strips(rows, work, carry):
    def step(k, c):
        return work(pl.ds(pl.multiple_of(k * STRIP, STRIP), STRIP), c)

    return lax.fori_loop(0, rows // STRIP, step, carry)


def head_kernel(
    part_ref,
    ordered_ref,
    own_low,
    own_high,
    other_low,
    other_high,
    bias_one,
    weight_two,
    bias_two,
    weight_out,
    bias_out,
    grad_one,
    grad_two_weight,
    small,
    last,
    decoded_ref,
    act_one,
    act_two,
    grad_two,
    slope_one,
    slope_two,
    wide,
    *,
    classes,
    norm,
):
    rows, half = own_low.shape
    hidden = 2 * half
    lanes = weight_out.shape[1]

    def one(at, c):
        for k, (own_ref, other_ref) in enumerate(((own_low, other_low), (own_high, other_high))):
            columns = slice(k * half, (k + 1) * half)
            x = own_ref[at, :].astype(F32) + other_ref[at, :].astype(F32) + bias_one[:, columns]
            act, slope = unit_and_slope(x)
            act_one[at, columns] = act.astype(BF)
            slope_one[at, columns] = slope
        return c

    strips(rows, one, 0)
    wide[...] = jnp.dot(act_one[...], weight_two[...], preferred_element_type=F32)

    def two(at, c):
        act, slope = unit_and_slope(wide[at, :] + bias_two[...])
        act_two[at, :] = act.astype(BF)
        slope_two[at, :] = slope
        return c

    strips(rows, two, 0)
    out = jnp.dot(act_two[...], weight_out[...], preferred_element_type=F32) + bias_out[...]
    ordered = ordered_ref[...]
    aux = jnp.concatenate(
        [
            jnp.zeros((BOX - 8, rows), F32),
            ordered[8:16],
            ordered[0:8],
            jnp.zeros((lanes - BOX - 8, rows), F32),
        ]
    ).T
    lane = lax.broadcasted_iota(jnp.int32, (rows, lanes), 1)
    is_class = lane < classes
    is_box = (lane >= BOX) & (lane < BOX + 4)
    label = aux[:, BOX - 6 : BOX - 5]
    hit = (lane.astype(F32) == label).astype(F32)
    fore = (label < classes - 1.0).astype(F32)
    scores = jnp.where(is_class, out, -3.0e38)
    top = jnp.max(scores, axis=1, keepdims=True)
    powers = jnp.where(is_class, jnp.exp(scores - top), 0.0)
    total = jnp.sum(powers, axis=1, keepdims=True)
    chosen = jnp.sum(jnp.where(is_class, out * hit, 0.0), axis=1, keepdims=True)
    class_loss = jnp.sum(top + jnp.log(total) - chosen, axis=0, keepdims=True) / norm
    residue = out - aux
    size = jnp.abs(residue)
    huber = jnp.where(size < 1.0, 0.5 * residue * residue, size - 0.5)
    huber = jnp.sum(jnp.where(is_box, huber, 0.0), axis=1, keepdims=True) * fore
    box_loss = jnp.sum(huber, axis=0, keepdims=True) / norm
    grad_out = jnp.where(
        is_class,
        (powers / total - hit) / norm,
        jnp.where(is_box, fore * jnp.clip(residue, -1.0, 1.0) / norm, 0.0),
    ).astype(BF)
    bias_sums = jnp.sum(grad_out.astype(F32), axis=0, keepdims=True)
    last[...] = jnp.concatenate(
        [
            bias_sums,
            jnp.broadcast_to(class_loss, (1, lanes)),
            jnp.broadcast_to(box_loss, (1, lanes)),
            jnp.zeros((5, lanes), F32),
        ]
    )
    moves = out.T[BOX : BOX + 4]
    x1, y1, x2, y2 = (ordered[k : k + 1] for k in range(4, 8))
    width, height = x2 - x1, y2 - y1
    px = moves[0:1] / 10.0 * width + (x1 + 0.5 * width)
    py = moves[1:2] / 10.0 * height + (y1 + 0.5 * height)
    half_w = 0.5 * (jnp.exp(moves[2:3] / 5.0) * width)
    half_h = 0.5 * (jnp.exp(moves[3:4] / 5.0) * height)
    boxes = jnp.concatenate(
        [px - half_w, py - half_h, px + half_w, py + half_h, jnp.zeros((4, rows), F32)]
    )
    place = lax.broadcasted_iota(jnp.int32, (rows, rows), 0).astype(F32)
    back = (ordered_ref[16:17, :] == place).astype(F32)
    decoded_ref[...] = jnp.dot(
        boxes, back, precision=lax.Precision.HIGHEST, preferred_element_type=F32
    )
    wide[...] = lax.dot_general(
        grad_out, weight_out[...], (((1,), (1,)), ((), ())), preferred_element_type=F32
    )

    def three(at, c):
        g = (wide[at, :] * slope_two[at, :]).astype(BF)
        grad_two[at, :] = g
        g = g.astype(F32)
        return c + g[0:8] + g[8:16]

    bias_two_sum = strips(rows, three, jnp.zeros((8, hidden), F32))
    wide[...] = lax.dot_general(
        grad_two[...], weight_two[...], (((1,), (1,)), ((), ())), preferred_element_type=F32
    )

    def four(at, c):
        g = (wide[at, :] * slope_one[at, :]).astype(BF)
        grad_one[at, :] = g
        g = g.astype(F32)
        return c + g[0:8] + g[8:16]

    bias_one_sum = strips(rows, four, jnp.zeros((8, hidden), F32))
    part = grad_two_weight.shape[0]
    columns = pl.ds(pl.multiple_of(part_ref[0] * part, part), part)
    grad_two_weight[...] = lax.dot_general(
        act_one[:, columns], grad_two[...], (((0,), (0,)), ((), ())), preferred_element_type=F32
    ).astype(BF)
    products = lax.dot_general(
        grad_out, act_two[...], (((0,), (0,)), ((), ())), preferred_element_type=F32
    )
    sums = jnp.concatenate(
        [
            jnp.sum(bias_one_sum, axis=0, keepdims=True),
            jnp.sum(bias_two_sum, axis=0, keepdims=True),
            jnp.zeros((lanes - BOX - 10, hidden), F32),
        ]
    )
    small[...] = jnp.concatenate([products[: BOX + 8], sums]).astype(BF)


def head_pass(
    part, parts, ordered, own, other, bias_one, weight_two, bias_two, weight_out, bias_out, classes, norm
):
    rows, hidden = own[0].shape[0], 2 * own[0].shape[1]
    lanes = weight_out.shape[1]
    whole = pl.BlockSpec(memory_space=pltpu.VMEM)
    return pl.pallas_call(
        functools.partial(head_kernel, classes=classes, norm=norm),
        in_specs=[pl.BlockSpec(memory_space=pltpu.SMEM)] + [whole] * 10,
        out_specs=[whole] * 5,
        out_shape=[
            jax.ShapeDtypeStruct((rows, hidden), BF),
            jax.ShapeDtypeStruct((hidden // parts, hidden), BF),
            jax.ShapeDtypeStruct((lanes, hidden), BF),
            jax.ShapeDtypeStruct((8, lanes), F32),
            jax.ShapeDtypeStruct((8, rows), F32),
        ],
        scratch_shapes=[pltpu.VMEM((rows, hidden), BF)] * 3 + [pltpu.VMEM((rows, hidden), F32)] * 3,
        compiler_params=pltpu.CompilerParams(vmem_limit_bytes=VM),
        cost_estimate=pl.CostEstimate(
            flops=6 * rows * hidden * hidden, bytes_accessed=8 * rows * hidden, transcendentals=0
        ),
        name="head",
    )(part, ordered, *own, *other, bias_one, weight_two, bias_two, weight_out, bias_out)


def partners(stride):
    return [(k, k ^ stride) for k in range(lax.axis_size("roi"))]


def halve(sums, axis, stride, size, with_last=False):
    while size > 1:
        mine = (lax.axis_index("roi") // stride) % 2
        shape = sums.shape
        split = sums.reshape(shape[:axis] + (size // 2, 2) + shape[axis + 1 :])
        keep = lax.dynamic_index_in_dim(split, mine, axis + 1, False)
        send = lax.dynamic_index_in_dim(split, 1 - mine, axis + 1, False)
        come = lax.ppermute(send, "roi", partners(stride))
        sums = (keep.astype(F32) + come.astype(F32)).astype(BF)
        stride, size = 2 * stride, size // 2
    sums = lax.squeeze(sums, (axis,))
    return (sums, come) if with_last else sums


def add_up_everywhere(values):
    stride = 1
    while stride < lax.axis_size("roi"):
        values = values + lax.ppermute(values, "roi", partners(stride))
        stride *= 2
    return values


def row_parts(rows):
    unit = 8 if rows % 8 == 0 else 1
    units = rows // unit
    cuts = [0, units * 16 // 49, units * 29 // 49, units * 37 // 49]
    return [unit * (b - a) for a, b in zip(cuts, cuts[1:])]


def spread_out(mine):
    stride, axis, shape = lax.axis_size("roi") // 2, 0, mine.shape
    while stride:
        low = (lax.axis_index("roi") // stride) % 2 == 0
        come = lax.ppermute(mine, "roi", partners(stride))
        mine = jnp.stack([jnp.where(low, mine, come), jnp.where(low, come, mine)], axis)
        stride, axis = stride // 2, axis + 1
    return mine.reshape(-1, shape[-1])


def after(value, *earlier):
    anywhere = pl.BlockSpec(memory_space=pl.ANY)
    return pl.pallas_call(
        lambda *refs: None,
        in_specs=[anywhere] * (1 + len(earlier)),
        out_specs=anywhere,
        out_shape=jax.ShapeDtypeStruct(value.shape, value.dtype),
        input_output_aliases={0: 0},
        cost_estimate=pl.CostEstimate(flops=0, bytes_accessed=0, transcendentals=0),
        name="after",
    )(value, *earlier)


def join_kernel(core_ref, mine_ref, theirs_ref, *outs, split):
    regions = theirs_ref.shape[-1]
    at = 0
    for rows, out in zip(split, outs):
        out[0, :, :regions] = mine_ref[0, 0, at : at + rows]
        out[0, :, regions:] = theirs_ref[0, at : at + rows]
        at += rows


def join_regions(core, by_core, theirs, split):
    blocks, _, share, regions = by_core.shape
    return pl.pallas_call(
        functools.partial(join_kernel, split=split),
        grid_spec=pltpu.PrefetchScalarGridSpec(
            num_scalar_prefetch=1,
            grid=(blocks,),
            in_specs=[
                pl.BlockSpec((1, 1, share, regions), lambda k, c: (k, c[0], 0, 0)),
                pl.BlockSpec((1, share, regions), lambda k, c: (k, 0, 0)),
            ],
            out_specs=[
                pl.BlockSpec((1, rows, 2 * regions), lambda k, c: (k, 0, 0)) for rows in split
            ],
        ),
        out_shape=[
            jax.ShapeDtypeStruct((blocks, rows, 2 * regions), by_core.dtype) for rows in split
        ],
        compiler_params=pltpu.CompilerParams(vmem_limit_bytes=VM),
        cost_estimate=pl.CostEstimate(
            flops=0, bytes_accessed=8 * blocks * share * regions, transcendentals=0
        ),
        name="join_regions",
    )(core, by_core, theirs)


class Halving:
    def __init__(self, rows, inner_first, inner, outer):
        ways, y, z = 2, [], []
        while ways < 2 * inner:
            y.append((1, ways))
            ways *= 2
        while ways < 2 * inner * outer:
            z.append((0, ways))
            ways *= 2
        self.rounds = y + z if inner_first else z + y
        self.first = len(y) if inner_first else 0
        self.opened = 1 if inner_first else 0
        self.costs, size = [], [outer, inner]
        for axis, stride in self.rounds:
            size[axis] //= 2
            far = stride // (2 if axis else 2 * inner)
            self.costs.append(size[0] * size[1] * rows * far)
        self.done = 0

    def begin(self, sums):
        self.sums = sums

    def send(self, *earlier):
        axis, stride = self.rounds[self.done]
        mine = (lax.axis_index("roi") // stride) % 2
        shape = self.sums.shape
        split = self.sums.reshape(shape[:axis] + (shape[axis] // 2, 2) + shape[axis + 1 :])
        self.keep = lax.dynamic_index_in_dim(split, mine, axis + 1, False)
        send = lax.dynamic_index_in_dim(split, 1 - mine, axis + 1, False)
        if earlier:
            send = after(send, *earlier)
        self.come = lax.ppermute(send, "roi", partners(stride))
        return send

    def add(self, *earlier):
        come = after(self.come, *earlier) if earlier else self.come
        self.sums = (self.keep.astype(F32) + come.astype(F32)).astype(BF)
        self.done += 1

    def result(self):
        return self.sums.reshape(self.sums.shape[-2:])


def arrival_order(parts):
    free, ready, order = {}, [0] * len(parts), []
    left = [list(enumerate(zip(p.rounds, p.costs))) for p in parts]
    while any(left):
        best, held = None, False
        opens = any(r and r[0][0] < p.first for r, p in zip(left, parts))
        for k, rounds in enumerate(left):
            if rounds:
                opening = rounds[0][0] < parts[k].first
                if opening and held or opens and rounds[0][1][0][0] > parts[k].opened:
                    continue
                held = held or opening
                number, ((axis, stride), cost) = rounds[0]
                link = "inner" if axis else stride
                start = max(ready[k], free.get(link, 0))
                if best is None or start + cost < best[0]:
                    best = (start + cost, k, number, link)
        end, k, number, link = best
        left[k].pop(0)
        ready[k] = free[link] = end
        order.append((k, number))
    return order


ROWS_AT_ONCE = 56


def widen_kernel(rows_ref, out_ref):
    out_ref[...] = rows_ref[...].astype(F32)


def widen_rows(rows):
    ways, count, hidden = rows.shape
    block = pl.BlockSpec((ways // 2, ROWS_AT_ONCE, hidden), lambda w, k: (w, k, 0))
    return pl.pallas_call(
        widen_kernel,
        grid=(2, count // ROWS_AT_ONCE),
        in_specs=[block],
        out_specs=block,
        out_shape=jax.ShapeDtypeStruct((ways, count, hidden), F32),
        compiler_params=pltpu.CompilerParams(vmem_limit_bytes=VM),
        cost_estimate=pl.CostEstimate(
            flops=0, bytes_accessed=6 * ways * count * hidden, transcendentals=0
        ),
        name="widen_rows",
    )(rows)


def on_device(
    pyramid_two,
    pyramid_three,
    pyramid_four,
    pyramid_five,
    proposals,
    image_index,
    levels,
    labels,
    targets,
    first_weight,
    first_bias,
    second_weight,
    second_bias,
    class_weight,
    class_bias,
    box_weight,
    box_bias,
):
    features = (pyramid_two, pyramid_three, pyramid_four, pyramid_five)
    images_here, channels_here = (pyramid_two.shape[0], pyramid_two.shape[1])
    regions_here = proposals.shape[1]
    ways, groups = lax.axis_size("roi"), lax.axis_size("ch")
    outer, inner = 4, ways // 8
    flat, hidden = first_weight.shape
    classes = class_weight.shape[1]
    share = flat // ways
    core = lax.axis_index("roi") % 2
    group = lax.axis_index("ch")
    maps = [f.reshape(images_here * channels_here, -1) for f in features]
    place = lax.axis_index("roi")
    base = jnp.stack([place * images_here, core]).astype(jnp.int32)
    pooled, send, ordered = pool_forward(
        base, proposals, targets, image_index[None], levels[None], labels[None], maps, channels_here
    )
    own, other = [], []
    for k in range(2):
        columns = slice(k * hidden // 2, (k + 1) * hidden // 2)
        partial = lax.dot_general(
            pooled, first_weight[:, columns], (((0,), (0,)), ((), ())), preferred_element_type=F32
        )
        if groups == 2:
            partial = partial.astype(BF)
            other.append(lax.ppermute(partial, "ch", [(0, 1), (1, 0)]))
        else:
            partial = lax.psum(partial, "ch")
            other.append(jnp.zeros(partial.shape, BF))
        own.append(partial)
    core = jnp.reshape(core, (1,)).astype(jnp.int32)
    by_core = pooled.reshape(ways // 2, 2, share, regions_here)
    theirs = lax.ppermute(send, "roi", partners(1))
    split = row_parts(share)
    both = join_regions(core, by_core, theirs, split)
    aside = share - sum(split)
    rows_aside = by_core[:, :, share - aside :].reshape(-1, regions_here)
    gap = jnp.zeros((hidden, BOX - classes), BF)
    tail = jnp.zeros((hidden, 128 - BOX - 4), BF)
    weight_out = jnp.concatenate([class_weight, gap, box_weight, tail], 1)
    bias_out = jnp.concatenate([class_bias, gap[0], box_bias, tail[0]]).astype(F32)[None]
    grad_pre_one, grad_two, small, last, decoded = head_pass(
        jnp.reshape(group, (1,)).astype(jnp.int32),
        groups,
        after(ordered, both[0]),
        own,
        other,
        first_bias.astype(F32)[None],
        second_weight,
        second_bias.astype(F32)[None],
        weight_out,
        bias_out,
        classes,
        float(regions_here * ways),
    )
    grad_both = jnp.concatenate([grad_pre_one, lax.ppermute(grad_pre_one, "roi", partners(1))], 0)
    part_aside = jnp.dot(rows_aside, grad_pre_one, preferred_element_type=F32).astype(BF)
    sum_aside = lax.psum_scatter(part_aside, "roi", tiled=True)
    order = [len(split) - 1] + list(range(len(split) - 1))
    halvings = [
        Halving(
            split[k] + ((hidden // groups + 128) // ways if k == len(split) - 2 else 0),
            k < len(split) - 1,
            inner,
            outer,
        )
        for k in order
    ]
    token, waiting = None, []
    for k, halving in zip(order, halvings):
        rows_both = both[k] if token is None else after(both[k], token)
        part = jnp.dot(
            rows_both.reshape(-1, 2 * regions_here), grad_both, preferred_element_type=F32
        )
        part = part.astype(BF).reshape(outer, inner, -1, hidden)
        token = part
        if k == len(split) - 2:
            extra = jnp.concatenate([after(grad_two, halvings[0].come), small])
            extra_share = extra.shape[0] // ways
            extra = halve(extra.reshape(ways // 2, 2, extra_share, hidden), 1, 1, 2)
            extra = extra.reshape(outer, inner, extra_share, hidden)
            part = jnp.concatenate([part, extra], 2)
        halving.begin(part)
        if len(waiting) == 0 or k == len(split) - 1:
            token = halving.send()
        if k == 0:
            token = halvings[0].come
        if k < len(split) - 1:
            waiting.append(halving)
    waiting = waiting[1:] + [halvings[0]]
    token = None
    for k, number in arrival_order(halvings):
        halving = halvings[k]
        come = halving.come
        halving.add(*(() if token is None else (token,)))
        more = number + 1 < len(halving.rounds)
        if number + 1 == halving.first:
            following = waiting.pop(0)
            if following.first or following.rounds[following.done][0] == 1:
                token = following.send(come)
        if more and not (halving in waiting and halving.rounds[number + 1][0] == 1):
            token = halving.send()
    sums = {k: h.result() for k, h in zip(order, halvings)}
    extra = sums[len(split) - 2][split[-2] :]
    sums[len(split) - 2] = sums[len(split) - 2][: split[-2]]
    share_sum = jnp.concatenate([sums[k] for k in range(len(split))] + [sum_aside])
    grad_weight_one = lax.all_gather(share_sum, "roi")
    if share % ROWS_AT_ONCE == 0:
        grad_weight_one = widen_rows(grad_weight_one)
    else:
        grad_weight_one = grad_weight_one.astype(F32)
    grad_weight_one = grad_weight_one.reshape(flat, hidden)
    extra = spread_out(extra)
    part_rows = hidden // groups
    small = extra[part_rows:].astype(F32)
    if groups == 2:
        two = extra[:part_rows]
        two_other = lax.ppermute(two, "ch", [(0, 1), (1, 0)])
        two = jnp.concatenate(
            [jnp.where(group == 0, two, two_other), jnp.where(group == 0, two_other, two)]
        )
    else:
        two = lax.all_gather(extra[:part_rows], "ch", tiled=True)
    grad_pooled = lax.dot_general(
        first_weight, grad_pre_one, (((1,), (1,)), ((), ())), preferred_element_type=F32
    ).astype(BF)
    last = add_up_everywhere(last)
    share_rows = regions_here // groups
    decoded = lax.dynamic_slice(decoded, (0, group * share_rows), (4, share_rows))
    map_grads = pool_backward(ordered, grad_pooled, channels_here)
    pyramid_grads = [g.reshape(f.shape) for g, f in zip(map_grads, features)]
    return (
        last[1, 0],
        last[2, 0],
        decoded,
        grad_weight_one,
        small[BOX + 8],
        two.astype(F32),
        small[BOX + 9],
        small[:classes].T,
        last[0, :classes],
        small[BOX : BOX + 4].T,
        last[0, BOX : BOX + 4],
        pyramid_grads[0],
        pyramid_grads[1],
        pyramid_grads[2],
        pyramid_grads[3],
    )


def solution(mesh):
    return jax.shard_map(
        on_device,
        mesh=mesh,
        in_specs=(
            P("roi", "ch", None),
            P("roi", "ch", None),
            P("roi", "ch", None),
            P("roi", "ch", None),
            P(None, "roi"),
            P("roi"),
            P("roi"),
            P("roi"),
            P(None, "roi"),
            P("ch", None),
            P(),
            P(),
            P(),
            P(),
            P(),
            P(),
            P(),
        ),
        out_specs=(
            P(),
            P(),
            P(None, ("roi", "ch")),
            P("ch", None),
            P(),
            P(),
            P(),
            P(),
            P(),
            P(),
            P(),
            P("roi", "ch", None),
            P("roi", "ch", None),
            P("roi", "ch", None),
            P("roi", "ch", None),
        ),
        check_vma=False,
    )
```
